512 devices in a mesh: expert: 128 (over y, z, core), dp: 4 (over x).
Axes of the slice: x: 4, y: 8, z: 8, core: 2. Of those that a mesh axis runs over, the one named last changes fastest.
Arguments:
- tokens: bfloat16 [16384, 2048], P('expert'), may hold values from -6 to 6
- routes: int32 [16384, 2], P('expert'), may hold values from 0 to 127, as said below
- route_weights: float32 [16384, 2], P('expert'), may hold values from 0.1 to 0.9
- loss_weights: float32 [16384], P('expert'), may hold values from 0.3 to 3
- gate_up: bfloat16 [128, 2, 768, 2048], P('expert', None, 'dp'), may hold values from -0.125 to 0.125
- down_weight: bfloat16 [128, 768, 2048], P('expert', 'dp'), may hold values from -0.21875 to 0.21875
Outputs:
- input_gradient: bfloat16 [16384, 2048], P('expert')
- projection_gradient: bfloat16 [128, 2, 768, 2048], P('expert', None, 'dp')
The draws below stay inside these ranges and needn't reach their ends.
Inputs may be any that keep to these rules, and one draw needn't show every extreme that they name: `routes`: each row names 2 different experts. One expert, the same for all rows, is named by exactly 4 rows of every aligned block of 128 rows (the tokens of one index of expert); every other expert is named by at most 2 rows of such a block, and some expert by exactly 2 rows of every block.
All inputs are finite; a program needn't handle non-finite values.
Results may differ from the reference program's by a relative error of at most 0.018.
Values may be sent and summed in bfloat16 or wider, within the bound.
No kernel may reach another device: no remote copies, remote signals or barrier semaphores. Data moves between devices by JAX's collectives and lax.ppermute only.
A program may use at most 64 MiB of HBM per device.

```python
import math
import jax
import jax.numpy as jnp
from jax import lax

D = 2048
F = 768
TOP = 2
TOK = 128
EXPERTS = 128
TOKENS = 16384
HOT_ROWS = 4
CAPC = 2
N_DP = 4


def draw_routes(key, part):
    key = jax.random.fold_in(key, 7)
    base_key, block_key = jax.random.split(key)
    ranking = jax.random.permutation(base_key, EXPERTS).astype(jnp.int32)
    busiest = ranking[0]
    designated = ranking[1]
    others = ranking[2:]
    blocks = TOKENS // TOK

    def one_block(block_seed):
        row_seed, list_seed, flip_seed = jax.random.split(block_seed, 3)
        shuffled = others[jax.random.permutation(list_seed, EXPERTS - 2).astype(jnp.int32)]
        cold_list = jnp.concatenate([designated[None], shuffled])
        spots = jnp.arange(TOK, dtype=jnp.int32)
        second = cold_list[spots % (EXPERTS - 1)]
        first = jnp.where(spots < HOT_ROWS, busiest, cold_list[(TOK + spots - HOT_ROWS) % (EXPERTS - 1)])
        flips = jax.random.randint(flip_seed, (TOK,), 0, 2)
        paired = jnp.stack([jnp.where(flips == 1, second, first), jnp.where(flips == 1, first, second)], axis=1)
        row_order = jax.random.permutation(row_seed, TOK).astype(jnp.int32)
        return jnp.zeros((TOK, TOP), jnp.int32).at[row_order].set(paired.astype(jnp.int32))
    return jax.vmap(one_block)(jax.random.split(block_key, blocks)).reshape(TOKENS, TOP)


def block_levels(stream_key, dims, cuts, least, largest):
    factor_of = 1.0
    for axis_at, blocks in cuts:
        draws = jax.random.uniform(jax.random.fold_in(jax.random.fold_in(stream_key, 6), axis_at), (blocks,), jnp.float32, least / len(cuts), largest / len(cuts))
        factor_of = factor_of * jnp.repeat(jnp.exp(draws), dims[axis_at] // blocks).reshape((-1,) + (1,) * (len(dims) - 1 - axis_at))
    return factor_of


def scatter_about(stream_key, dims, spread, reach, shards=(), kind=jnp.bfloat16):
    level = block_levels(stream_key, dims, shards, -0.22, 0.18) if shards else 1.0
    result = jax.random.normal(stream_key, dims, jnp.float32) * spread * level
    return jnp.minimum(jnp.maximum(result, -reach), reach).astype(kind)


def setup_inputs(seed: int = 0) -> dict:
    splits = jax.random.split(jax.random.key(seed), 7)
    return {
        "tokens": scatter_about(splits[0], (TOKENS, D), 1.0, 6.0, ((0, 128),)),
        "routes": draw_routes(jax.random.fold_in(splits[6], 71), 0),
        "route_weights": jnp.clip(0.1 + 0.79999997 * jax.random.uniform(splits[2], (TOKENS, TOP), jnp.float32) ** block_levels(splits[2], (TOKENS, TOP), ((0, 128),), -0.2, 0.2), 0.1, 0.9),
        "loss_weights": jnp.clip(jnp.exp(math.log(3.0) - 2.3025851 * jax.random.uniform(splits[3], (TOKENS,), jnp.float32) ** block_levels(splits[3], (TOKENS,), ((0, 128),), -0.2, 0.2)), 0.3, 3.0),
        "gate_up": scatter_about(splits[4], (EXPERTS, 2, F, D), D ** -0.5, 0.125, ((0, 128), (2, 4))),
        "down_weight": scatter_about(splits[5], (EXPERTS, F, D), F ** -0.5, 0.21875, ((0, 128), (1, 4))),
    }


def swish_parts(preact):
    sigmoid_part = jax.nn.sigmoid(preact)
    return preact * sigmoid_part, sigmoid_part * (1.0 + preact * (1.0 - sigmoid_part))


def rounded(amount):
    return lax.optimization_barrier(amount.astype(jnp.bfloat16)).astype(jnp.float32)


def expert_forward(row_block, weight_in, weight_out):
    quarter = F // N_DP
    running = jnp.zeros((row_block.shape[0], D), jnp.float32)
    for quarter_index in range(N_DP):
        window = weight_in[:, quarter_index * quarter:(quarter_index + 1) * quarter, :].reshape(2 * quarter, D)
        projected = jnp.dot(row_block, window.T, preferred_element_type=jnp.float32)
        swish_value, _ = swish_parts(projected[:, :quarter])
        hidden = (swish_value * projected[:, quarter:]).astype(jnp.bfloat16)
        lower_rows = weight_out[quarter_index * quarter:(quarter_index + 1) * quarter]
        running = running + rounded(jnp.dot(hidden, lower_rows, preferred_element_type=jnp.float32))
    return running.astype(jnp.bfloat16)


def expert_backward(row_block, cotangent, weight_in, weight_out):
    quarter = F // N_DP
    running = jnp.zeros((row_block.shape[0], D), jnp.float32)
    pieces = []
    for quarter_index in range(N_DP):
        window = weight_in[:, quarter_index * quarter:(quarter_index + 1) * quarter, :].reshape(2 * quarter, D)
        projected = jnp.dot(row_block, window.T, preferred_element_type=jnp.float32)
        swish_value, swish_slope = swish_parts(projected[:, :quarter])
        lower_rows = weight_out[quarter_index * quarter:(quarter_index + 1) * quarter]
        back_hidden = jnp.dot(cotangent, lower_rows.T, preferred_element_type=jnp.float32)
        grad_pre = jnp.concatenate([back_hidden * projected[:, quarter:] * swish_slope, back_hidden * swish_value], axis=1).astype(jnp.bfloat16)
        pieces.append(jnp.dot(grad_pre.T, row_block, preferred_element_type=jnp.float32).reshape(2, quarter, D))
        running = running + rounded(jnp.dot(grad_pre, window, preferred_element_type=jnp.float32))
    return running.astype(jnp.bfloat16), jnp.concatenate(pieces, axis=1)


def reference(tokens, routes, route_weights, loss_weights, gate_up, down_weight):
    count = TOKENS * TOP
    flat_routes = routes.reshape(count).astype(jnp.int32)
    owners = (jnp.arange(count, dtype=jnp.int32) // TOP).astype(jnp.int32)
    counts = jnp.sum((flat_routes[:, None] == jnp.arange(EXPERTS, dtype=jnp.int32)[None, :]).astype(jnp.int32), axis=0)
    busiest = jnp.argmax(counts).astype(jnp.int32)
    sorted_order = jnp.argsort(flat_routes, stable=True).astype(jnp.int32)
    starts = (jnp.cumsum(counts) - counts).astype(jnp.int32)
    cold_cap = CAPC * EXPERTS
    hot_cap = HOT_ROWS * EXPERTS
    order_pad = jnp.concatenate([sorted_order, jnp.full((hot_cap,), count, jnp.int32)])
    owner_pad = jnp.concatenate([owners, jnp.zeros((1,), jnp.int32)])

    def select(expert, capacity, allowed):
        picked = lax.dynamic_slice(order_pad, (starts[expert].astype(jnp.int32),), (capacity,))
        usable = (jnp.arange(capacity, dtype=jnp.int32) < counts[expert]) & allowed
        picked = jnp.where(usable, picked, count).astype(jnp.int32)
        row_block = jnp.where(usable[:, None], tokens[owner_pad[picked]], jnp.zeros((), jnp.bfloat16))
        return picked, row_block

    def forward_one(expert):
        picked, row_block = select(expert, cold_cap, expert != busiest)
        return picked, expert_forward(row_block, gate_up[expert], down_weight[expert])

    cold_picked, cold_out = lax.map(forward_one, jnp.arange(EXPERTS, dtype=jnp.int32))
    hot_picked, hot_block = select(busiest, hot_cap, busiest == busiest)
    hot_out = expert_forward(hot_block, gate_up[busiest], down_weight[busiest])
    every_picked = jnp.concatenate([cold_picked.reshape(-1), hot_picked])
    every_out = jnp.concatenate([cold_out.reshape(-1, D), hot_out])
    expert_out = jnp.zeros((count + 1, D), jnp.bfloat16).at[every_picked].set(every_out)[:count]
    expert_out = expert_out.reshape(TOKENS, TOP, D).astype(jnp.float32)
    combined = jnp.sum(route_weights[:, :, None] * expert_out, axis=1)
    cotangent = (loss_weights[:, None, None] * route_weights[:, :, None] * combined[:, None, :]).astype(jnp.bfloat16).reshape(count, D)
    cot_pad = jnp.concatenate([cotangent, jnp.zeros((1, D), jnp.bfloat16)])

    def backward_one(expert):
        picked, row_block = select(expert, cold_cap, expert != busiest)
        input_each, gradient = expert_backward(row_block, cot_pad[picked], gate_up[expert], down_weight[expert])
        return picked, input_each, gradient.astype(jnp.bfloat16)

    cold_picked, cold_input, cold_grads = lax.map(backward_one, jnp.arange(EXPERTS, dtype=jnp.int32))
    hot_input, hot_grad = expert_backward(hot_block, cot_pad[hot_picked], gate_up[busiest], down_weight[busiest])
    every_input = jnp.concatenate([cold_input.reshape(-1, D), hot_input])
    input_each = jnp.zeros((count + 1, D), jnp.bfloat16).at[every_picked].set(every_input)[:count]
    input_gradient = jnp.sum(input_each.reshape(TOKENS, TOP, D).astype(jnp.float32), axis=1).astype(jnp.bfloat16)
    projection_gradient = cold_grads.at[busiest].set(hot_grad.astype(jnp.bfloat16))
    return input_gradient, projection_gradient
```

```python
import jax
import jax.numpy as jnp
from jax import lax
from jax.experimental import pallas as pl
from jax.experimental.pallas import tpu as pltpu
from jax.sharding import PartitionSpec as P

BF = jnp.bfloat16
F32 = jnp.float32
SLOTS = 4
VMEM_BYTES = 48 * 1024 * 1024


def swish_parts(preact):
    sigmoid_part = jax.nn.sigmoid(preact)
    return (preact * sigmoid_part, sigmoid_part * (1.0 + preact * (1.0 - sigmoid_part)))


def over_experts(rows):
    return lax.all_to_all(rows, "expert", split_axis=0, concat_axis=0, tiled=True)


def over_dp(blocks):
    return lax.all_to_all(blocks, "dp", split_axis=0, concat_axis=0, tiled=True)


def gather_columns(block):
    parts = lax.axis_size("dp")
    return over_dp(jnp.broadcast_to(block[None], (parts,) + block.shape))


def dot_t(a, b):
    return lax.dot_general(a, b, (((1,), (1,)), ((), ())), preferred_element_type=F32)


def forward_kernel(rows_ref, win_ref, wout_ref, part_ref, proj_ref):
    parts, _, cols = rows_ref.shape
    quarter = wout_ref.shape[0]
    projected = dot_t(rows_ref[0], win_ref[:, :cols])
    for q in range(1, parts):
        projected += dot_t(rows_ref[q], win_ref[:, q * cols : (q + 1) * cols])
    proj_ref[...] = projected
    swish_value, _ = swish_parts(projected[:, :quarter])
    hidden = (swish_value * projected[:, quarter:]).astype(BF)
    for q in range(parts):
        part_ref[q] = jnp.dot(
            hidden, wout_ref[:, q * cols : (q + 1) * cols], preferred_element_type=F32
        ).astype(BF)


def backward_kernel(rows_ref, cot_ref, proj_ref, win_ref, wout_ref, part_ref, grad_ref):
    parts, _, cols = rows_ref.shape
    quarter = wout_ref.shape[0]
    back_hidden = dot_t(cot_ref[0], wout_ref[:, :cols])
    for q in range(1, parts):
        back_hidden += dot_t(cot_ref[q], wout_ref[:, q * cols : (q + 1) * cols])
    projected = proj_ref[...]
    swish_value, swish_slope = swish_parts(projected[:, :quarter])
    grad_pre = jnp.concatenate(
        [back_hidden * projected[:, quarter:] * swish_slope, back_hidden * swish_value], axis=1
    ).astype(BF)
    for q in range(parts):
        span = slice(q * cols, (q + 1) * cols)
        part_ref[q] = jnp.dot(grad_pre, win_ref[:, span], preferred_element_type=F32).astype(BF)
        grad_ref[:, span] = lax.dot_general(
            grad_pre, rows_ref[q], (((0,), (0,)), ((), ())), preferred_element_type=F32
        ).astype(BF)


def local(tokens, routes, route_weights, loss_weights, gate_up, down_weight):
    experts = lax.axis_size("expert")
    parts = lax.axis_size("dp")
    width = tokens.shape[1]
    cols = width // parts
    local_tokens = tokens.shape[0]
    choices = routes.shape[1]
    quarter = down_weight.shape[1]
    assignments = local_tokens * choices
    slots = experts * SLOTS
    params = pltpu.CompilerParams(vmem_limit_bytes=VMEM_BYTES)
    own_in = gate_up.reshape(2 * quarter, width)
    own_out = down_weight.reshape(quarter, width)

    flat = routes.T.reshape(assignments)
    member = (flat[:, None] == lax.iota(jnp.int32, experts)[None, :]).astype(BF)
    positions = lax.iota(jnp.int32, assignments)
    earlier = (positions[None, :] < positions[:, None]).astype(BF)
    rank_table = jnp.dot(earlier, member, preferred_element_type=F32)
    rank = jnp.sum(rank_table * member.astype(F32), axis=1).astype(jnp.int32)
    slot_index = (flat * SLOTS + rank).reshape(choices, local_tokens)
    slot_ids = lax.iota(jnp.int32, slots)
    place = (slot_ids[None, :, None] == slot_index[:, None, :]).astype(BF)
    pick = (slot_index[:, :, None] == slot_ids[None, None, :]).astype(BF)

    mine = lax.dynamic_slice(
        tokens, (jnp.int32(0), lax.axis_index("dp") * cols), (local_tokens, cols)
    )
    outgoing = jnp.dot(place[0] + place[1], mine, preferred_element_type=F32).astype(BF)
    rows = gather_columns(over_experts(outgoing))

    partial, projected = pl.pallas_call(
        forward_kernel,
        out_shape=(
            jax.ShapeDtypeStruct((parts, slots, cols), BF),
            jax.ShapeDtypeStruct((slots, 2 * quarter), F32),
        ),
        compiler_params=params,
    )(rows, own_in, own_out)
    expert_out = jnp.sum(over_dp(partial).astype(F32), axis=0).astype(BF)
    returned = over_experts(expert_out)

    combined = sum(
        route_weights[:, k : k + 1] * jnp.dot(pick[k], returned, preferred_element_type=F32)
        for k in range(choices)
    )
    cot_send = sum(
        jnp.dot(
            place[k],
            (loss_weights[:, None] * route_weights[:, k : k + 1] * combined).astype(BF),
            preferred_element_type=F32,
        )
        for k in range(choices)
    ).astype(BF)
    cot = gather_columns(over_experts(cot_send))

    input_partial, gradient = pl.pallas_call(
        backward_kernel,
        out_shape=(
            jax.ShapeDtypeStruct((parts, slots, cols), BF),
            jax.ShapeDtypeStruct((2 * quarter, width), BF),
        ),
        compiler_params=params,
    )(rows, cot, projected, own_in, own_out)
    input_each = jnp.sum(over_dp(input_partial).astype(F32), axis=0).astype(BF)
    returned_in = over_experts(input_each)
    input_quarter = jnp.dot(
        pick[0] + pick[1], returned_in, preferred_element_type=F32
    ).astype(BF)
    gathered = gather_columns(input_quarter)
    input_gradient = jnp.swapaxes(gathered, 0, 1).reshape(local_tokens, width)
    return (input_gradient, gradient.reshape(1, 2, quarter, width))


def solution(mesh):
    in_specs = (
        P("expert", None),
        P("expert", None),
        P("expert", None),
        P("expert"),
        P("expert", None, "dp", None),
        P("expert", "dp", None),
    )
    out_specs = (P("expert", None), P("expert", None, "dp", None))
    return jax.shard_map(local, mesh=mesh, in_specs=in_specs, out_specs=out_specs, check_vma=False)
```

```python
import functools

import jax
import jax.numpy as jnp
from jax import lax
from jax.experimental import pallas as pl
from jax.experimental.pallas import tpu as pltpu
from jax.sharding import PartitionSpec as P

BF = jnp.bfloat16
F32 = jnp.float32
SLOTS = 3
LANES = 128
VMEM_BYTES = 48 * 1024 * 1024
VMEM = pl.BlockSpec(memory_space=pltpu.VMEM)
SMEM = pl.BlockSpec(memory_space=pltpu.SMEM)


def swish_parts(preact):
    sigmoid_part = jax.nn.sigmoid(preact)
    return (preact * sigmoid_part, sigmoid_part * (1.0 + preact * (1.0 - sigmoid_part)))


def over_experts(rows):
    count, cols = rows.shape
    experts = lax.axis_size("expert")
    blocks = rows.reshape(experts, count // experts, cols // LANES, LANES)
    moved = lax.all_to_all(blocks, "expert", split_axis=0, concat_axis=0, tiled=True)
    return moved.reshape(count, cols)


def shift_dp(block, step):
    parts = lax.axis_size("dp")
    return lax.ppermute(block, "dp", [(i, (i + step) % parts) for i in range(parts)])


def gather_dp(block):
    return [block] + [shift_dp(block, k) for k in range(1, lax.axis_size("dp"))]


def scatter_sum_dp(blocks):
    total = blocks[0].astype(F32)
    for moved in [shift_dp(blocks[k], k) for k in range(1, len(blocks))]:
        total = total + moved.astype(F32)
    return total.astype(BF)


def swap_cores(value):
    experts = lax.axis_size("expert")
    return lax.ppermute(value, "expert", [(i, i ^ 1) for i in range(experts)])


def mm(a, b):
    return jnp.dot(a, b, preferred_element_type=F32)


def mm_t(a, b):
    return lax.dot_general(a, b, (((1,), (1,)), ((), ())), preferred_element_type=F32)


def t_mm(a, b):
    return lax.dot_general(a, b, (((0,), (0,)), ((), ())), preferred_element_type=F32)


def span_of(where_ref, step, cols, parts):
    block = lax.rem(where_ref[0] + (step + parts), parts)
    return pl.ds(pl.multiple_of(block * cols, cols), cols)


def extra_rows(shape):
    return lax.rem(lax.broadcasted_iota(jnp.int32, shape, 0), SLOTS) == SLOTS - 1


def contract(blocks, weight_ref, where_ref):
    parts = len(blocks)
    cols = blocks[0].shape[1]
    total = None
    for k in range(parts):
        term = mm_t(blocks[k][...], weight_ref[:, span_of(where_ref, -k, cols, parts)])
        total = term if total is None else total + term
    return total


def expand(value, weight_ref, other_ref, where_ref, outs):
    parts = len(outs)
    cols = outs[0].shape[1]

    @pl.when(where_ref[1] == 0)
    def _():
        for k in range(parts):
            span = span_of(where_ref, k, cols, parts)
            outs[k][...] = mm(value, weight_ref[:, span]).astype(BF)

    @pl.when(where_ref[1] != 0)
    def _():
        extra = extra_rows(value.shape)
        mine = jnp.where(extra, jnp.zeros_like(value), value)
        theirs = jnp.where(extra, value, jnp.zeros_like(value))
        for k in range(parts):
            span = span_of(where_ref, k, cols, parts)
            outs[k][...] = (mm(mine, weight_ref[:, span]) + mm(theirs, other_ref[:, span])).astype(
                BF
            )


def forward_kernel(parts, where_ref, *refs):
    rows = refs[:parts]
    win_ref, wout_ref, other_in_ref, other_out_ref = refs[parts : parts + 4]
    outs = refs[parts + 4 : 2 * parts + 4]
    proj_ref = refs[2 * parts + 4]
    quarter = wout_ref.shape[0]
    proj_ref[...] = contract(rows, win_ref, where_ref)

    @pl.when(where_ref[1] != 0)
    def _():
        other = contract(rows, other_in_ref, where_ref)
        proj_ref[...] = jnp.where(extra_rows(other.shape), other, proj_ref[...])

    projected = proj_ref[...]
    swish_value, _ = swish_parts(projected[:, :quarter])
    hidden = (swish_value * projected[:, quarter:]).astype(BF)
    expand(hidden, wout_ref, other_out_ref, where_ref, outs)


def backward_kernel(parts, where_ref, *refs):
    cots = refs[:parts]
    proj_ref, win_ref, wout_ref, other_in_ref, other_out_ref = refs[parts : parts + 5]
    outs = refs[parts + 5 : 2 * parts + 5]
    grad_pre_ref, back_ref = refs[2 * parts + 5 :]
    quarter = wout_ref.shape[0]
    back_ref[...] = contract(cots, wout_ref, where_ref)

    @pl.when(where_ref[1] != 0)
    def _():
        other = contract(cots, other_out_ref, where_ref)
        back_ref[...] = jnp.where(extra_rows(other.shape), other, back_ref[...])

    back_hidden = back_ref[...]
    projected = proj_ref[...]
    swish_value, swish_slope = swish_parts(projected[:, :quarter])
    grad_pre = jnp.concatenate(
        [back_hidden * projected[:, quarter:] * swish_slope, back_hidden * swish_value], axis=1
    ).astype(BF)
    grad_pre_ref[...] = grad_pre
    expand(grad_pre, win_ref, other_in_ref, where_ref, outs)


def other_gradient_kernel(parts, where_ref, *refs):
    rows = refs[:parts]
    grad_pre_ref, out_ref = refs[parts:]
    cols = rows[0].shape[1]

    @pl.when(where_ref[1] == 0)
    def _():
        out_ref[...] = jnp.zeros_like(out_ref)

    @pl.when(where_ref[1] != 0)
    def _():
        grad_pre = grad_pre_ref[...]
        theirs = jnp.where(extra_rows(grad_pre.shape), grad_pre, jnp.zeros_like(grad_pre))
        for k in range(parts):
            span = span_of(where_ref, -k, cols, parts)
            out_ref[:, span] = t_mm(theirs, rows[k][...]).astype(BF)


def gradient_kernel(parts, where_ref, *refs):
    rows = refs[:parts]
    grad_pre_ref, other_ref, out_ref = refs[parts:]
    cols = rows[0].shape[1]
    grad_pre = grad_pre_ref[...]
    skip = extra_rows(grad_pre.shape) & (where_ref[1] != 0)
    mine = jnp.where(skip, jnp.zeros_like(grad_pre), grad_pre)
    for k in range(parts):
        span = span_of(where_ref, -k, cols, parts)
        out_ref[:, span] = (t_mm(mine, rows[k][...]) + other_ref[:, span].astype(F32)).astype(BF)


def one_hot(slot_ref, k, slots):
    shape = (slot_ref.shape[0], slots)
    return (lax.broadcasted_iota(jnp.int32, shape, 1) == slot_ref[:, k : k + 1]).astype(BF)


def send_kernel(slot_ref, tokens_ref, out_ref):
    slots = out_ref.shape[0]
    both = sum(one_hot(slot_ref, k, slots) for k in range(slot_ref.shape[1]))
    out_ref[...] = t_mm(both, tokens_ref[...]).astype(BF)


def combine_kernel(slot_ref, route_weight_ref, loss_weight_ref, returned_ref, out_ref):
    slots = out_ref.shape[0]
    choices = slot_ref.shape[1]
    picks = [one_hot(slot_ref, k, slots) for k in range(choices)]
    weights = [route_weight_ref[:, k : k + 1] for k in range(choices)]
    returned = returned_ref[...]
    combined = sum(weights[k] * mm(picks[k], returned) for k in range(choices))
    loss = loss_weight_ref[...]
    out_ref[...] = sum(
        t_mm(picks[k], (loss * weights[k] * combined).astype(BF)) for k in range(choices)
    ).astype(BF)


def collect_kernel(slot_ref, returned_ref, out_ref):
    slots = returned_ref.shape[0]
    both = sum(one_hot(slot_ref, k, slots) for k in range(slot_ref.shape[1]))
    out_ref[...] = mm(both, returned_ref[...]).astype(BF)


def join_kernel(parts, where_ref, *refs):
    out_ref = refs[parts]
    cols = refs[0].shape[1]
    for k in range(parts):
        out_ref[:, span_of(where_ref, -k, cols, parts)] = refs[k][...]


def call(kernel, outs, args, scalars=1, scratch=()):
    return pl.pallas_call(
        kernel,
        out_shape=outs,
        in_specs=[SMEM] * scalars + [VMEM] * (len(args) - scalars),
        out_specs=jax.tree.map(lambda _: VMEM, outs),
        scratch_shapes=list(scratch),
        compiler_params=pltpu.CompilerParams(vmem_limit_bytes=VMEM_BYTES),
    )(*args)


def local(tokens, routes, route_weights, loss_weights, gate_up, down_weight):
    experts = lax.axis_size("expert")
    parts = lax.axis_size("dp")
    part = lax.axis_index("dp")
    index = lax.axis_index("expert")
    local_tokens, width = tokens.shape
    cols = width // parts
    choices = routes.shape[1]
    quarter = down_weight.shape[1]
    assignments = local_tokens * choices
    slots = experts * SLOTS
    own_in = gate_up.reshape(2 * quarter, width)
    own_out = down_weight.reshape(quarter, width)

    flat = routes.reshape(assignments)
    member = (flat[:, None] == lax.iota(jnp.int32, experts)[None, :]).astype(BF)
    busiest = jnp.argmax(jnp.sum(member.astype(F32), axis=0)).astype(jnp.int32)
    positions = lax.iota(jnp.int32, assignments)
    earlier = (positions[None, :] < positions[:, None]).astype(BF)
    rank = jnp.sum(mm(earlier, member) * member.astype(F32), axis=1).astype(jnp.int32)
    slot = jnp.where(
        rank == SLOTS, (flat ^ 1) * SLOTS + SLOTS - 1, flat * SLOTS + rank
    ).reshape(local_tokens, choices)
    where = jnp.stack([part, ((index ^ 1) == busiest).astype(jnp.int32)]).astype(jnp.int32)

    block = jax.ShapeDtypeStruct((slots, cols), BF)
    mine = lax.dynamic_slice(tokens, (jnp.int32(0), part * cols), (local_tokens, cols))
    outgoing = call(send_kernel, block, (slot, mine), scalars=0)
    rows = gather_dp(over_experts(outgoing))
    other_in, other_out = swap_cores(own_in), swap_cores(own_out)

    *partial, projected = call(
        functools.partial(forward_kernel, parts),
        [block] * parts + [jax.ShapeDtypeStruct((slots, 2 * quarter), F32)],
        (where, *rows, own_in, own_out, other_in, other_out),
    )
    returned = over_experts(scatter_sum_dp(partial))

    cot_send = call(
        combine_kernel,
        block,
        (slot, route_weights, loss_weights.reshape(local_tokens, 1), returned),
        scalars=0,
    )
    cots = gather_dp(over_experts(cot_send))

    *input_partial, grad_pre = call(
        functools.partial(backward_kernel, parts),
        [block] * parts + [jax.ShapeDtypeStruct((slots, 2 * quarter), BF)],
        (where, *cots, projected, own_in, own_out, other_in, other_out),
        scratch=[pltpu.VMEM((slots, quarter), F32)],
    )
    returned_in = over_experts(scatter_sum_dp(input_partial))

    whole_gradient = jax.ShapeDtypeStruct((2 * quarter, width), BF)
    lent = call(
        functools.partial(other_gradient_kernel, parts), whole_gradient, (where, *rows, grad_pre)
    )
    gradient = call(
        functools.partial(gradient_kernel, parts),
        whole_gradient,
        (where, *rows, grad_pre, swap_cores(lent)),
    )

    collected = call(
        collect_kernel,
        jax.ShapeDtypeStruct((local_tokens, cols), BF),
        (slot, returned_in),
        scalars=0,
    )
    input_gradient = call(
        functools.partial(join_kernel, parts),
        jax.ShapeDtypeStruct((local_tokens, width), BF),
        (where, *gather_dp(collected)),
    )
    return (input_gradient, gradient.reshape(1, 2, quarter, width))


def solution(mesh):
    in_specs = (
        P("expert", None),
        P("expert", None),
        P("expert", None),
        P("expert"),
        P("expert", None, "dp", None),
        P("expert", "dp", None),
    )
    out_specs = (P("expert", None), P("expert", None, "dp", None))
    return jax.shard_map(local, mesh=mesh, in_specs=in_specs, out_specs=out_specs, check_vma=False)
```

```python
import functools

import jax
import jax.numpy as jnp
from jax import lax
from jax.experimental import pallas as pl
from jax.experimental.pallas import tpu as pltpu
from jax.sharding import PartitionSpec as P

BF = jnp.bfloat16
F32 = jnp.float32
CORES = 2
SLOTS = 3
LANES = 128
VMEM_BYTES = 20 * 1024 * 1024
VMEM = pl.BlockSpec(memory_space=pltpu.VMEM)
SMEM = pl.BlockSpec(memory_space=pltpu.SMEM)
ANY = pl.BlockSpec(memory_space=pl.ANY)


def swish_parts(preact):
    sigmoid_part = jax.nn.sigmoid(preact)
    return (preact * sigmoid_part, sigmoid_part * (1.0 + preact * (1.0 - sigmoid_part)))


def over_chips(rows):
    count, cols = rows.shape
    experts = lax.axis_size("expert")
    chips = experts // CORES
    moved = lax.all_to_all(
        rows.reshape(chips, CORES * SLOTS, cols // LANES, LANES),
        "expert",
        split_axis=0,
        concat_axis=0,
        tiled=True,
        axis_index_groups=[list(range(core, experts, CORES)) for core in range(CORES)],
    )
    return moved.reshape(count, cols)


def over_dp(blocks):
    return lax.all_to_all(blocks, "dp", split_axis=0, concat_axis=0, tiled=True)


def gather_dp(block):
    return over_dp(jnp.broadcast_to(block[None], (lax.axis_size("dp"),) + block.shape))


def sum_dp(blocks):
    moved = over_dp(blocks)
    total = moved[0].astype(F32)
    for q in range(1, moved.shape[0]):
        total = total + moved[q].astype(F32)
    return total.astype(BF)


def swap_cores(value):
    experts = lax.axis_size("expert")
    return lax.ppermute(value, "expert", [(i, i ^ 1) for i in range(experts)])


def mm(a, b):
    return jnp.dot(a, b, preferred_element_type=F32)


def mm_t(a, b):
    return lax.dot_general(a, b, (((1,), (1,)), ((), ())), preferred_element_type=F32)


def t_mm(a, b):
    return lax.dot_general(a, b, (((0,), (0,)), ((), ())), preferred_element_type=F32)


def column_blocks(ref):
    parts, _, cols = ref.shape
    return [(q, slice(q * cols, (q + 1) * cols)) for q in range(parts)]


def rows_of_core(where_ref, shape, core):
    row = lax.broadcasted_iota(jnp.int32, shape, 0)
    at = (lax.rem(row, CORES * SLOTS) >= SLOTS).astype(jnp.int32)
    hot_core = jnp.where(where_ref[1] == 1, where_ref[0], 1 - where_ref[0])
    lent = (lax.rem(row, SLOTS) == SLOTS - 1) & (where_ref[1] != 0)
    return jnp.where(lent, hot_core, at) == core


def contract(blocks_ref, own_ref, other_ref, where_ref):
    def product(weight_ref):
        return sum(mm_t(blocks_ref[q], weight_ref[:, span]) for q, span in column_blocks(blocks_ref))

    own = product(own_ref)
    return jnp.where(rows_of_core(where_ref, own.shape, where_ref[0]), own, product(other_ref))


def expand(value, own_ref, other_ref, where_ref, out_ref):
    owned = rows_of_core(where_ref, value.shape, where_ref[0])
    mine = jnp.where(owned, value, jnp.zeros_like(value))
    theirs = jnp.where(owned, jnp.zeros_like(value), value)
    for q, span in column_blocks(out_ref):
        out_ref[q] = (mm(mine, own_ref[:, span]) + mm(theirs, other_ref[:, span])).astype(BF)


def forward_kernel(
    where_ref, rows_ref, in_ref, out_ref, other_in_ref, other_out_ref, partial_ref, proj_ref
):
    quarter = out_ref.shape[0]
    projected = contract(rows_ref, in_ref, other_in_ref, where_ref)
    proj_ref[...] = projected
    swish_value, _ = swish_parts(projected[:, :quarter])
    hidden = (swish_value * projected[:, quarter:]).astype(BF)
    expand(hidden, out_ref, other_out_ref, where_ref, partial_ref)


def backward_kernel(
    where_ref, cot_ref, proj_ref, in_ref, out_ref, other_in_ref, other_out_ref, partial_ref, pre_ref
):
    quarter = out_ref.shape[0]
    back_hidden = contract(cot_ref, out_ref, other_out_ref, where_ref)
    projected = proj_ref[...]
    swish_value, swish_slope = swish_parts(projected[:, :quarter])
    grad_pre = jnp.concatenate(
        [back_hidden * projected[:, quarter:] * swish_slope, back_hidden * swish_value], axis=1
    ).astype(BF)
    pre_ref[...] = grad_pre
    expand(grad_pre, in_ref, other_in_ref, where_ref, partial_ref)


def lent_gradient_kernel(where_ref, rows_ref, pre_ref, out_ref):
    pre = pre_ref[...]
    owned = rows_of_core(where_ref, pre.shape, where_ref[0])
    theirs = jnp.where(owned, jnp.zeros_like(pre), pre)
    for q, span in column_blocks(rows_ref):
        out_ref[:, span] = t_mm(theirs, rows_ref[q]).astype(BF)


def gradient_kernel(where_ref, rows_ref, pre_ref, lent_ref, out_ref):
    pre = pre_ref[...]
    owned = rows_of_core(where_ref, pre.shape, where_ref[0])
    mine = jnp.where(owned, pre, jnp.zeros_like(pre))
    for q, span in column_blocks(rows_ref):
        out_ref[:, span] = (t_mm(mine, rows_ref[q]) + lent_ref[:, span].astype(F32)).astype(BF)


def places(slot_ref, slots):
    shape = (slots, slot_ref.shape[1])
    row = lax.broadcasted_iota(jnp.int32, shape, 0)
    return [(row == slot_ref[k : k + 1, :]).astype(BF) for k in range(slot_ref.shape[0])]


def send_kernel(experts, routes_ref, tokens_ref, slot_ref, busiest_ref, out_ref):
    choices, local_tokens = routes_ref.shape
    square = (local_tokens, local_tokens)
    earlier = (
        lax.broadcasted_iota(jnp.int32, square, 0) < lax.broadcasted_iota(jnp.int32, square, 1)
    ).astype(BF)
    ids = lax.broadcasted_iota(jnp.int32, (experts, local_tokens), 0)
    counts = jnp.zeros((experts, 1), F32)
    for k in range(choices):
        expert = routes_ref[k : k + 1, :]
        member = ids == expert
        before = mm(member.astype(BF), earlier) + counts
        rank = jnp.sum(jnp.where(member, before, 0.0), axis=0, keepdims=True).astype(jnp.int32)
        counts += jnp.sum(member.astype(F32), axis=1, keepdims=True)
        slot_ref[k : k + 1, :] = jnp.where(
            rank == SLOTS, (expert ^ 1) * SLOTS + SLOTS - 1, expert * SLOTS + rank
        )
    most = jnp.max(counts, axis=0, keepdims=True)
    ids = lax.broadcasted_iota(jnp.int32, counts.shape, 0).astype(F32)
    busiest = jnp.sum(jnp.where(counts == most, ids, 0.0), axis=0, keepdims=True)
    busiest_ref[...] = busiest.astype(jnp.int32)
    both = sum(places(slot_ref, out_ref.shape[0]))
    out_ref[...] = mm(both, tokens_ref[...]).astype(BF)


def combine_kernel(slot_ref, route_weight_ref, loss_weight_ref, returned_ref, out_ref):
    place = places(slot_ref, out_ref.shape[0])
    choices = len(place)
    weights = [route_weight_ref[:, k : k + 1] for k in range(choices)]
    returned = returned_ref[...]
    combined = sum(weights[k] * t_mm(place[k], returned) for k in range(choices))
    loss = loss_weight_ref[...]
    out_ref[...] = sum(
        mm(place[k], (loss * weights[k] * combined).astype(BF)) for k in range(choices)
    ).astype(BF)


def collect_kernel(slot_ref, returned_ref, out_ref):
    both = sum(places(slot_ref, returned_ref.shape[0]))
    collected = t_mm(both, returned_ref[...]).astype(BF)
    for q in range(out_ref.shape[0]):
        out_ref[q] = collected


def join_kernel(parts_ref, _, out_ref):
    for q, span in column_blocks(parts_ref):
        out_ref[:, span] = parts_ref[q]


def call(kernel, outs, args, scalars=0, after=()):
    return pl.pallas_call(
        kernel,
        out_shape=outs,
        in_specs=[SMEM] * scalars + [VMEM] * (len(args) - scalars) + [ANY] * len(after),
        out_specs=jax.tree.map(lambda _: VMEM, outs),
        compiler_params=pltpu.CompilerParams(vmem_limit_bytes=VMEM_BYTES),
    )(*args, *after)


def local(tokens, routes, route_weights, loss_weights, gate_up, down_weight):
    experts = lax.axis_size("expert")
    parts = lax.axis_size("dp")
    index = lax.axis_index("expert")
    local_tokens, width = tokens.shape
    cols = width // parts
    choices = routes.shape[1]
    quarter = down_weight.shape[1]
    slots = experts * SLOTS
    own_in = gate_up.reshape(2 * quarter, width)
    own_out = down_weight.reshape(quarter, width)

    def out(*shape, dtype=BF):
        return jax.ShapeDtypeStruct(shape, dtype)

    mine = lax.dynamic_slice(
        tokens, (jnp.int32(0), lax.axis_index("dp") * cols), (local_tokens, cols)
    )
    slot, busiest, outgoing = call(
        functools.partial(send_kernel, experts),
        [out(choices, local_tokens, dtype=jnp.int32), out(1, 1, dtype=jnp.int32), out(slots, cols)],
        (routes.T, mine),
    )
    busiest = busiest[0, 0]
    hot = jnp.where(busiest == index, 1, jnp.where(busiest == (index ^ 1), 2, 0))
    where = jnp.stack([index & 1, hot]).astype(jnp.int32)

    other_in, other_out = swap_cores(own_in), swap_cores(own_out)
    weights = (own_in, own_out, other_in, other_out)
    rows = gather_dp(over_chips(outgoing))
    partial, projected = call(
        forward_kernel,
        [out(parts, slots, cols), out(slots, 2 * quarter, dtype=F32)],
        (where, rows, *weights),
        scalars=1,
    )
    returned = over_chips(sum_dp(partial))
    cot_send = call(
        combine_kernel,
        out(slots, cols),
        (slot, route_weights, loss_weights.reshape(local_tokens, 1), returned),
    )
    cot = gather_dp(over_chips(cot_send))
    input_partial, grad_pre = call(
        backward_kernel,
        [out(parts, slots, cols), out(slots, 2 * quarter)],
        (where, cot, projected, *weights),
        scalars=1,
    )
    lent = call(
        lent_gradient_kernel, out(2 * quarter, width), (where, rows, grad_pre), scalars=1
    )
    gradient = call(
        gradient_kernel,
        out(2 * quarter, width),
        (where, rows, grad_pre, swap_cores(lent)),
        scalars=1,
    )
    returned_in = over_chips(sum_dp(input_partial))
    collected = call(
        collect_kernel, out(parts, local_tokens, cols), (slot, returned_in)
    )
    input_gradient = call(
        join_kernel,
        out(local_tokens, width),
        (over_dp(collected),),
        after=(gradient,),
    )
    return (input_gradient, gradient.reshape(1, 2, quarter, width))


def solution(mesh):
    in_specs = (
        P("expert", None),
        P("expert", None),
        P("expert", None),
        P("expert"),
        P("expert", None, "dp", None),
        P("expert", "dp", None),
    )
    out_specs = (P("expert", None), P("expert", None, "dp", None))
    return jax.shard_map(local, mesh=mesh, in_specs=in_specs, out_specs=out_specs, check_vma=False)
```

```python
import functools

import jax
import jax.numpy as jnp
from jax import lax
from jax.experimental import pallas as pl
from jax.experimental.pallas import tpu as pltpu
from jax.sharding import PartitionSpec as P

BF = jnp.bfloat16
F32 = jnp.float32
CORES = 2
SLOTS = 3
LANES = 128
VMEM_BYTES = 20 * 1024 * 1024
VMEM = pl.BlockSpec(memory_space=pltpu.VMEM)
SMEM = pl.BlockSpec(memory_space=pltpu.SMEM)
HBM = pl.BlockSpec(memory_space=pltpu.HBM)


def swish_parts(preact):
    sigmoid_part = jax.nn.sigmoid(preact)
    return (preact * sigmoid_part, sigmoid_part * (1.0 + preact * (1.0 - sigmoid_part)))


def over_chips(rows):
    count = rows.shape[0]
    cols = rows.size // count
    experts = lax.axis_size("expert")
    chips = experts // CORES
    moved = lax.all_to_all(
        rows.reshape(chips, CORES * SLOTS, cols // LANES, LANES),
        "expert",
        split_axis=0,
        concat_axis=0,
        tiled=True,
        axis_index_groups=[list(range(core, experts, CORES)) for core in range(CORES)],
    )
    return moved.reshape(count, cols)


def over_dp(blocks):
    return lax.all_to_all(blocks, "dp", split_axis=0, concat_axis=0, tiled=True)


def gather_dp(block):
    return over_dp(jnp.broadcast_to(block[None], (lax.axis_size("dp"),) + block.shape))


def sum_dp(blocks):
    moved = over_dp(blocks)
    total = moved[0].astype(F32)
    for q in range(1, moved.shape[0]):
        total = total + moved[q].astype(F32)
    return total.astype(BF)


def swap_cores(value):
    experts = lax.axis_size("expert")
    return lax.ppermute(value, "expert", [(i, i ^ 1) for i in range(experts)])


def mm(a, b):
    return jnp.dot(a, b, preferred_element_type=F32)


def mm_t(a, b):
    return lax.dot_general(a, b, (((1,), (1,)), ((), ())), preferred_element_type=F32)


def t_mm(a, b):
    return lax.dot_general(a, b, (((0,), (0,)), ((), ())), preferred_element_type=F32)


def column_blocks(ref):
    parts, _, cols = ref.shape
    return [(q, slice(q * cols, (q + 1) * cols)) for q in range(parts)]


def rows_of_core(where_ref, shape, core):
    row = lax.broadcasted_iota(jnp.int32, shape, 0)
    at = (lax.rem(row, CORES * SLOTS) >= SLOTS).astype(jnp.int32)
    hot_core = jnp.where(where_ref[1] == 1, where_ref[0], 1 - where_ref[0])
    lent = (lax.rem(row, SLOTS) == SLOTS - 1) & (where_ref[1] != 0)
    return jnp.where(lent, hot_core, at) == core


def fetch(sources, targets, sems):
    copies = [
        pltpu.make_async_copy(source, target, sems.at[i])
        for i, (source, target) in enumerate(zip(sources, targets))
    ]
    for copy in copies:
        copy.start()
    return [copy.wait for copy in copies]


def contract(blocks_ref, own_ref, other_ref, where_ref, own_here, other_here):
    def product(weight_ref):
        return sum(mm_t(blocks_ref[q], weight_ref[:, span]) for q, span in column_blocks(blocks_ref))

    own_here()
    own = product(own_ref)
    other_here()
    other = product(other_ref)
    return jnp.where(rows_of_core(where_ref, own.shape, where_ref[0]), own, other)


def expand(value, own_ref, other_ref, where_ref, out_ref, done=lambda q: None):
    owned = rows_of_core(where_ref, value.shape, where_ref[0])
    mine = jnp.where(owned, value, jnp.zeros_like(value))
    theirs = jnp.where(owned, jnp.zeros_like(value), value)
    for q, span in column_blocks(out_ref):
        out_ref[q] = (mm(mine, own_ref[:, span]) + mm(theirs, other_ref[:, span])).astype(BF)
        done(q)


def forward_kernel(where_ref, rows_ref, *refs):
    sources, (partial_ref, proj_ref), held, sems = refs[:4], refs[4:6], refs[6:10], refs[10]
    in_ref, other_in_ref, out_ref, other_out_ref = held
    in_here, other_in_here, out_here, other_out_here = fetch(sources, held, sems)
    quarter = out_ref.shape[0]
    projected = contract(rows_ref, in_ref, other_in_ref, where_ref, in_here, other_in_here)
    proj_ref[...] = projected
    swish_value, _ = swish_parts(projected[:, :quarter])
    hidden = (swish_value * projected[:, quarter:]).astype(BF)
    out_here()
    other_out_here()
    expand(hidden, out_ref, other_out_ref, where_ref, partial_ref)


def backward_kernel(where_ref, cot_ref, proj_ref, *refs):
    sources, (partial_ref, pre_ref), held, sems = refs[:4], refs[4:6], refs[6:10], refs[10]
    block_ref, block_sems = refs[11:]
    out_ref, other_out_ref, in_ref, other_in_ref = held
    out_here, other_out_here, in_here, other_in_here = fetch(sources, held, sems)
    quarter = out_ref.shape[0]
    back_hidden = contract(cot_ref, out_ref, other_out_ref, where_ref, out_here, other_out_here)
    projected = proj_ref[...]
    swish_value, swish_slope = swish_parts(projected[:, :quarter])
    grad_pre = jnp.concatenate(
        [back_hidden * projected[:, quarter:] * swish_slope, back_hidden * swish_value], axis=1
    ).astype(BF)
    pre_ref[...] = grad_pre
    in_here()
    other_in_here()
    sent = []

    def send(q):
        copy = pltpu.make_async_copy(block_ref.at[q], partial_ref.at[q], block_sems.at[q])
        copy.start()
        sent.append(copy)

    expand(grad_pre, in_ref, other_in_ref, where_ref, block_ref, send)
    for copy in sent:
        copy.wait()


def lent_gradient_kernel(where_ref, rows_ref, pre_ref, out_ref):
    pre = pre_ref[...]
    owned = rows_of_core(where_ref, pre.shape, where_ref[0])
    theirs = jnp.where(owned, jnp.zeros_like(pre), pre)
    for q, span in column_blocks(rows_ref):
        out_ref[:, span] = t_mm(theirs, rows_ref[q]).astype(BF)


def gradient_kernel(where_ref, rows_ref, pre_ref, lent_ref, out_ref, done_ref):
    pre = pre_ref[...]
    owned = rows_of_core(where_ref, pre.shape, where_ref[0])
    mine = jnp.where(owned, pre, jnp.zeros_like(pre))
    for q, span in column_blocks(rows_ref):
        out_ref[:, span] = (t_mm(mine, rows_ref[q]) + lent_ref[:, span].astype(F32)).astype(BF)
    done_ref[...] = jnp.zeros_like(done_ref)


def places(slot_ref, slots):
    shape = (slots, slot_ref.shape[1])
    row = lax.broadcasted_iota(jnp.int32, shape, 0)
    return [(row == slot_ref[k : k + 1, :]).astype(BF) for k in range(slot_ref.shape[0])]


def send_kernel(
    experts, part_ref, routes_ref, tokens_ref, slot_ref, busiest_ref, out_ref, held_ref, sem
):
    choices, local_tokens = routes_ref.shape
    cols = held_ref.shape[1]
    span = pl.ds(pl.multiple_of(part_ref[0] * cols, cols), cols)
    copy = pltpu.make_async_copy(tokens_ref.at[:, span], held_ref, sem)
    copy.start()
    square = (local_tokens, local_tokens)
    earlier = (
        lax.broadcasted_iota(jnp.int32, square, 0) < lax.broadcasted_iota(jnp.int32, square, 1)
    ).astype(BF)
    ids = lax.broadcasted_iota(jnp.int32, (experts, local_tokens), 0)
    counts = jnp.zeros((experts, 1), F32)
    for k in range(choices):
        expert = routes_ref[k : k + 1, :]
        member = ids == expert
        before = mm(member.astype(BF), earlier) + counts
        rank = jnp.sum(jnp.where(member, before, 0.0), axis=0, keepdims=True).astype(jnp.int32)
        counts += jnp.sum(member.astype(F32), axis=1, keepdims=True)
        slot_ref[k : k + 1, :] = jnp.where(
            rank == SLOTS, (expert ^ 1) * SLOTS + SLOTS - 1, expert * SLOTS + rank
        )
    most = jnp.max(counts, axis=0, keepdims=True)
    ids = lax.broadcasted_iota(jnp.int32, counts.shape, 0).astype(F32)
    busiest = jnp.sum(jnp.where(counts == most, ids, 0.0), axis=0, keepdims=True)
    busiest_ref[...] = busiest.astype(jnp.int32)
    both = sum(places(slot_ref, out_ref.shape[0]))
    copy.wait()
    out_ref[...] = mm(both, held_ref[...]).astype(BF).reshape(out_ref.shape)


def combine_kernel(slot_ref, route_weight_ref, loss_weight_ref, returned_ref, out_ref):
    place = places(slot_ref, out_ref.shape[0])
    choices = len(place)
    weights = [route_weight_ref[:, k : k + 1] for k in range(choices)]
    returned = returned_ref[...]
    combined = sum(weights[k] * t_mm(place[k], returned) for k in range(choices))
    loss = loss_weight_ref[...]
    out_ref[...] = sum(
        mm(place[k], (loss * weights[k] * combined).astype(BF)) for k in range(choices)
    ).astype(BF).reshape(out_ref.shape)


def collect_kernel(slot_ref, returned_ref, out_ref):
    both = sum(places(slot_ref, returned_ref.shape[0]))
    collected = t_mm(both, returned_ref[...]).astype(BF)
    for q in range(out_ref.shape[0]):
        out_ref[q] = collected


def join_kernel(parts_ref, done_ref, out_ref):
    del done_ref
    for q, span in column_blocks(parts_ref):
        out_ref[:, span] = parts_ref[q]


def call(kernel, outs, args, ins=None, out_specs=None, scratch=()):
    return pl.pallas_call(
        kernel,
        out_shape=outs,
        in_specs=ins or [VMEM] * len(args),
        out_specs=out_specs or jax.tree.map(lambda _: VMEM, outs),
        scratch_shapes=list(scratch),
        compiler_params=pltpu.CompilerParams(vmem_limit_bytes=VMEM_BYTES),
    )(*args)


def local(tokens, routes, route_weights, loss_weights, gate_up, down_weight):
    experts = lax.axis_size("expert")
    parts = lax.axis_size("dp")
    index = lax.axis_index("expert")
    local_tokens, width = tokens.shape
    cols = width // parts
    choices = routes.shape[1]
    quarter = down_weight.shape[1]
    slots = experts * SLOTS
    own_in = gate_up.reshape(2 * quarter, width)
    own_out = down_weight.reshape(quarter, width)

    def out(*shape, dtype=BF):
        return jax.ShapeDtypeStruct(shape, dtype)

    dma = pltpu.SemaphoreType.DMA
    sent = out(slots, cols // LANES, LANES)
    slot, busiest, outgoing = call(
        functools.partial(send_kernel, experts),
        [out(choices, local_tokens, dtype=jnp.int32), out(1, 1, dtype=jnp.int32), sent],
        (lax.axis_index("dp").reshape(1), routes.T, tokens),
        ins=[SMEM, VMEM, HBM],
        scratch=[pltpu.VMEM((local_tokens, cols), BF), dma],
    )
    busiest = busiest[0, 0]
    hot = jnp.where(busiest == index, 1, jnp.where(busiest == (index ^ 1), 2, 0))
    where = jnp.stack([index & 1, hot]).astype(jnp.int32)

    other_in, other_out = swap_cores(own_in), swap_cores(own_out)
    held = [pltpu.VMEM(w.shape, BF) for w in (own_in, own_in, own_out, own_out)]
    rows = gather_dp(over_chips(outgoing))
    partial, projected = call(
        forward_kernel,
        [out(parts, slots, cols), out(slots, 2 * quarter, dtype=F32)],
        (where, rows, own_in, other_in, own_out, other_out),
        ins=[SMEM, VMEM] + [HBM] * 4,
        scratch=[*held, dma((4,))],
    )
    returned = over_chips(sum_dp(partial))
    cot_send = call(
        combine_kernel,
        sent,
        (slot, route_weights, loss_weights.reshape(local_tokens, 1), returned),
    )
    cot = gather_dp(over_chips(cot_send))
    input_partial, grad_pre = call(
        backward_kernel,
        [out(parts, slots, cols), out(slots, 2 * quarter)],
        (where, cot, projected, own_out, other_out, own_in, other_in),
        ins=[SMEM, VMEM, VMEM] + [HBM] * 4,
        out_specs=[HBM, VMEM],
        scratch=[*held[2:], *held[:2], dma((4,)), pltpu.VMEM((parts, slots, cols), BF), dma((parts,))],
    )
    lent = call(
        lent_gradient_kernel,
        out(2 * quarter, width),
        (where, rows, grad_pre),
        ins=[SMEM, VMEM, VMEM],
    )
    gradient, gradient_done = call(
        gradient_kernel,
        [out(2 * quarter, width), out(8, LANES, dtype=F32)],
        (where, rows, grad_pre, swap_cores(lent)),
        ins=[SMEM, VMEM, VMEM, VMEM],
    )
    returned_in = over_chips(sum_dp(input_partial))
    collected = call(
        collect_kernel, out(parts, local_tokens, cols), (slot, returned_in)
    )
    input_gradient = call(
        join_kernel, out(local_tokens, width), (over_dp(collected), gradient_done)
    )
    return (input_gradient, gradient.reshape(1, 2, quarter, width))


def solution(mesh):
    in_specs = (
        P("expert", None),
        P("expert", None),
        P("expert", None),
        P("expert"),
        P("expert", None, "dp", None),
        P("expert", "dp", None),
    )
    out_specs = (P("expert", None), P("expert", None, "dp", None))
    return jax.shard_map(local, mesh=mesh, in_specs=in_specs, out_specs=out_specs, check_vma=False)
```

```python
import functools

import jax
import jax.numpy as jnp
from jax import lax
from jax.experimental import pallas as pl
from jax.experimental.pallas import tpu as pltpu
from jax.sharding import PartitionSpec as P

BF = jnp.bfloat16
F32 = jnp.float32
CORES = 2
SLOTS = 3
LANES = 128
VMEM_BYTES = 20 * 1024 * 1024
VMEM = pl.BlockSpec(memory_space=pltpu.VMEM)
SMEM = pl.BlockSpec(memory_space=pltpu.SMEM)


def swish_parts(preact):
    sigmoid_part = jax.nn.sigmoid(preact)
    return (preact * sigmoid_part, sigmoid_part * (1.0 + preact * (1.0 - sigmoid_part)))


def over_chips(rows):
    count = rows.shape[0]
    cols = rows.size // count
    experts = lax.axis_size("expert")
    chips = experts // CORES
    moved = lax.all_to_all(
        rows.reshape(chips, CORES * SLOTS, cols // LANES, LANES),
        "expert",
        split_axis=0,
        concat_axis=0,
        tiled=True,
        axis_index_groups=[list(range(core, experts, CORES)) for core in range(CORES)],
    )
    return moved.reshape(count, cols)


def over_dp(blocks):
    return lax.all_to_all(blocks, "dp", split_axis=0, concat_axis=0, tiled=True)


def gather_dp(block):
    return over_dp(jnp.broadcast_to(block[None], (lax.axis_size("dp"),) + block.shape))


def swap_cores(value):
    experts = lax.axis_size("expert")
    return lax.ppermute(value, "expert", [(i, i ^ 1) for i in range(experts)])


def mm(a, b):
    return jnp.dot(a, b, preferred_element_type=F32)


def mm_t(a, b):
    return lax.dot_general(a, b, (((1,), (1,)), ((), ())), preferred_element_type=F32)


def t_mm(a, b):
    return lax.dot_general(a, b, (((0,), (0,)), ((), ())), preferred_element_type=F32)


def column_blocks(ref):
    parts, _, cols = ref.shape
    return [(q, slice(q * cols, (q + 1) * cols)) for q in range(parts)]


def rows_of_core(where_ref, shape, core):
    row = lax.broadcasted_iota(jnp.int32, shape, 0)
    at = (lax.rem(row, CORES * SLOTS) >= SLOTS).astype(jnp.int32)
    hot_core = jnp.where(where_ref[1] == 1, where_ref[0], 1 - where_ref[0])
    lent = (lax.rem(row, SLOTS) == SLOTS - 1) & (where_ref[1] != 0)
    return jnp.where(lent, hot_core, at) == core


def contract(blocks_ref, own_ref, other_ref, where_ref):
    def product(weight_ref):
        return sum(mm_t(blocks_ref[q], weight_ref[:, span]) for q, span in column_blocks(blocks_ref))

    own = product(own_ref)
    return jnp.where(rows_of_core(where_ref, own.shape, where_ref[0]), own, product(other_ref))


def expand(value, own_ref, other_ref, where_ref, out_ref):
    owned = rows_of_core(where_ref, value.shape, where_ref[0])
    mine = jnp.where(owned, value, jnp.zeros_like(value))
    theirs = jnp.where(owned, jnp.zeros_like(value), value)
    for q, span in column_blocks(out_ref):
        out_ref[q] = (mm(mine, own_ref[:, span]) + mm(theirs, other_ref[:, span])).astype(BF)


def forward_kernel(
    where_ref, rows_ref, in_ref, out_ref, other_in_ref, other_out_ref, partial_ref, proj_ref
):
    quarter = out_ref.shape[0]
    projected = contract(rows_ref, in_ref, other_in_ref, where_ref)
    proj_ref[...] = projected
    swish_value, _ = swish_parts(projected[:, :quarter])
    hidden = (swish_value * projected[:, quarter:]).astype(BF)
    expand(hidden, out_ref, other_out_ref, where_ref, partial_ref)


def backward_kernel(
    where_ref, cot_ref, proj_ref, in_ref, out_ref, other_in_ref, other_out_ref, partial_ref, pre_ref
):
    quarter = out_ref.shape[0]
    back_hidden = contract(cot_ref, out_ref, other_out_ref, where_ref)
    projected = proj_ref[...]
    swish_value, swish_slope = swish_parts(projected[:, :quarter])
    grad_pre = jnp.concatenate(
        [back_hidden * projected[:, quarter:] * swish_slope, back_hidden * swish_value], axis=1
    ).astype(BF)
    pre_ref[...] = grad_pre
    expand(grad_pre, in_ref, other_in_ref, where_ref, partial_ref)


def lent_gradient_kernel(where_ref, rows_ref, pre_ref, out_ref):
    pre = pre_ref[...]
    owned = rows_of_core(where_ref, pre.shape, where_ref[0])
    theirs = jnp.where(owned, jnp.zeros_like(pre), pre)
    for q, span in column_blocks(rows_ref):
        out_ref[:, span] = t_mm(theirs, rows_ref[q]).astype(BF)


def gradient_kernel(where_ref, rows_ref, pre_ref, lent_ref, out_ref, done_ref):
    pre = pre_ref[...]
    owned = rows_of_core(where_ref, pre.shape, where_ref[0])
    mine = jnp.where(owned, pre, jnp.zeros_like(pre))
    for q, span in column_blocks(rows_ref):
        out_ref[:, span] = (t_mm(mine, rows_ref[q]) + lent_ref[:, span].astype(F32)).astype(BF)
    done_ref[...] = jnp.zeros_like(done_ref)


def places(slot_ref, slots):
    shape = (slots, slot_ref.shape[1])
    row = lax.broadcasted_iota(jnp.int32, shape, 0)
    return [(row == slot_ref[k : k + 1, :]).astype(BF) for k in range(slot_ref.shape[0])]


def send_kernel(experts, routes_ref, tokens_ref, slot_ref, busiest_ref, out_ref):
    choices, local_tokens = routes_ref.shape
    square = (local_tokens, local_tokens)
    earlier = (
        lax.broadcasted_iota(jnp.int32, square, 0) < lax.broadcasted_iota(jnp.int32, square, 1)
    ).astype(BF)
    ids = lax.broadcasted_iota(jnp.int32, (experts, local_tokens), 0)
    counts = jnp.zeros((experts, 1), F32)
    for k in range(choices):
        expert = routes_ref[k : k + 1, :]
        member = ids == expert
        before = mm(member.astype(BF), earlier) + counts
        rank = jnp.sum(jnp.where(member, before, 0.0), axis=0, keepdims=True).astype(jnp.int32)
        counts += jnp.sum(member.astype(F32), axis=1, keepdims=True)
        slot_ref[k : k + 1, :] = jnp.where(
            rank == SLOTS, (expert ^ 1) * SLOTS + SLOTS - 1, expert * SLOTS + rank
        )
    most = jnp.max(counts, axis=0, keepdims=True)
    ids = lax.broadcasted_iota(jnp.int32, counts.shape, 0).astype(F32)
    busiest = jnp.sum(jnp.where(counts == most, ids, 0.0), axis=0, keepdims=True)
    busiest_ref[...] = busiest.astype(jnp.int32)
    both = sum(places(slot_ref, out_ref.shape[0]))
    out_ref[...] = mm(both, tokens_ref[...]).astype(BF).reshape(out_ref.shape)


def combine_kernel(slot_ref, route_weight_ref, loss_weight_ref, returned_ref, out_ref):
    place = places(slot_ref, out_ref.shape[0])
    choices = len(place)
    scales = jnp.transpose(
        jnp.concatenate(
            [route_weight_ref[...], loss_weight_ref[...], jnp.zeros((7 - choices, route_weight_ref.shape[1]), F32)], axis=0
        )
    )
    weights = [scales[:, k : k + 1] for k in range(choices)]
    returned = returned_ref[...]
    combined = sum(weights[k] * t_mm(place[k], returned) for k in range(choices))
    loss = scales[:, choices : choices + 1]
    out_ref[...] = sum(
        mm(place[k], (loss * weights[k] * combined).astype(BF)) for k in range(choices)
    ).astype(BF).reshape(out_ref.shape)


def collect_kernel(slot_ref, returned_ref, out_ref):
    both = sum(places(slot_ref, returned_ref.shape[0]))
    collected = t_mm(both, returned_ref[...]).astype(BF)
    for q in range(out_ref.shape[0]):
        out_ref[q] = collected


def join_kernel(parts_ref, done_ref, out_ref):
    del done_ref
    for q, span in column_blocks(parts_ref):
        out_ref[:, span] = parts_ref[q]


def sum_kernel(blocks_ref, out_ref):
    total = blocks_ref[0].astype(F32)
    for q in range(1, blocks_ref.shape[0]):
        total = total + blocks_ref[q].astype(F32)
    out_ref[...] = total.astype(BF).reshape(out_ref.shape)


def call(kernel, outs, args, scalars=0):
    return pl.pallas_call(
        kernel,
        out_shape=outs,
        in_specs=[SMEM] * scalars + [VMEM] * (len(args) - scalars),
        out_specs=jax.tree.map(lambda _: VMEM, outs),
        compiler_params=pltpu.CompilerParams(vmem_limit_bytes=VMEM_BYTES),
    )(*args)


def local(tokens, routes, route_weights, loss_weights, gate_up, down_weight):
    experts = lax.axis_size("expert")
    parts = lax.axis_size("dp")
    index = lax.axis_index("expert")
    local_tokens, width = tokens.shape
    cols = width // parts
    choices = routes.shape[1]
    quarter = down_weight.shape[1]
    slots = experts * SLOTS
    own_in = gate_up.reshape(2 * quarter, width)
    own_out = down_weight.reshape(quarter, width)

    def out(*shape, dtype=BF):
        return jax.ShapeDtypeStruct(shape, dtype)

    sent = out(slots, cols // LANES, LANES)
    mine = lax.dynamic_slice(
        tokens, (jnp.int32(0), lax.axis_index("dp") * cols), (local_tokens, cols)
    )
    slot, busiest, outgoing = call(
        functools.partial(send_kernel, experts),
        [out(choices, local_tokens, dtype=jnp.int32), out(1, 1, dtype=jnp.int32), sent],
        (routes.T, mine),
    )
    busiest = busiest[0, 0]
    hot = jnp.where(busiest == index, 1, jnp.where(busiest == (index ^ 1), 2, 0))
    where = jnp.stack([index & 1, hot]).astype(jnp.int32)

    other_in, other_out = swap_cores(own_in), swap_cores(own_out)
    weights = (own_in, own_out, other_in, other_out)
    rows = gather_dp(over_chips(outgoing))
    partial, projected = call(
        forward_kernel,
        [out(parts, slots, cols), out(slots, 2 * quarter, dtype=F32)],
        (where, rows, *weights),
        scalars=1,
    )
    returned = over_chips(call(sum_kernel, sent, (over_dp(partial),)))
    cot_send = call(
        combine_kernel,
        sent,
        (slot, route_weights.T, loss_weights.reshape(1, local_tokens), returned),
    )
    cot = gather_dp(over_chips(cot_send))
    input_partial, grad_pre = call(
        backward_kernel,
        [out(parts, slots, cols), out(slots, 2 * quarter)],
        (where, cot, projected, *weights),
        scalars=1,
    )
    lent = call(
        lent_gradient_kernel, out(2 * quarter, width), (where, rows, grad_pre), scalars=1
    )
    gradient, gradient_done = call(
        gradient_kernel,
        [out(2 * quarter, width), out(8, LANES, dtype=F32)],
        (where, rows, grad_pre, swap_cores(lent)),
        scalars=1,
    )
    returned_in = over_chips(call(sum_kernel, sent, (over_dp(input_partial),)))
    collected = call(
        collect_kernel, out(parts, local_tokens, cols), (slot, returned_in)
    )
    input_gradient = call(
        join_kernel, out(local_tokens, width), (over_dp(collected), gradient_done)
    )
    return (input_gradient, gradient.reshape(1, 2, quarter, width))


def solution(mesh):
    in_specs = (
        P("expert", None),
        P("expert", None),
        P("expert", None),
        P("expert"),
        P("expert", None, "dp", None),
        P("expert", "dp", None),
    )
    out_specs = (P("expert", None), P("expert", None, "dp", None))
    return jax.shard_map(local, mesh=mesh, in_specs=in_specs, out_specs=out_specs, check_vma=False)
```

```python
import functools

import jax
import jax.numpy as jnp
from jax import lax
from jax.experimental import pallas as pl
from jax.experimental.pallas import tpu as pltpu
from jax.sharding import PartitionSpec as P

BF = jnp.bfloat16
F32 = jnp.float32
CORES = 2
SLOTS = 3
LANES = 128
VMEM_BYTES = 20 * 1024 * 1024
VMEM = pl.BlockSpec(memory_space=pltpu.VMEM)
SMEM = pl.BlockSpec(memory_space=pltpu.SMEM)


def swish_parts(preact):
    sigmoid_part = jax.nn.sigmoid(preact)
    return (preact * sigmoid_part, sigmoid_part * (1.0 + preact * (1.0 - sigmoid_part)))


def over_chips(rows):
    count = rows.shape[0]
    cols = rows.size // count
    experts = lax.axis_size("expert")
    chips = experts // CORES
    moved = lax.all_to_all(
        rows.reshape(chips, CORES * SLOTS, cols // LANES, LANES),
        "expert",
        split_axis=0,
        concat_axis=0,
        tiled=True,
        axis_index_groups=[list(range(core, experts, CORES)) for core in range(CORES)],
    )
    return moved.reshape(count, cols)


def over_dp(blocks):
    return lax.all_to_all(blocks, "dp", split_axis=0, concat_axis=0, tiled=True)


def gather_dp(block):
    return over_dp(jnp.broadcast_to(block[None], (lax.axis_size("dp"),) + block.shape))


def swap_cores(value):
    experts = lax.axis_size("expert")
    return lax.ppermute(value, "expert", [(i, i ^ 1) for i in range(experts)])


def mm(a, b):
    return jnp.dot(a, b, preferred_element_type=F32)


def mm_t(a, b):
    return lax.dot_general(a, b, (((1,), (1,)), ((), ())), preferred_element_type=F32)


def t_mm(a, b):
    return lax.dot_general(a, b, (((0,), (0,)), ((), ())), preferred_element_type=F32)


def column_blocks(ref):
    parts, _, cols = ref.shape
    return [(q, slice(q * cols, (q + 1) * cols)) for q in range(parts)]


def rows_of_core(where_ref, shape, core):
    row = lax.broadcasted_iota(jnp.int32, shape, 0)
    at = (lax.rem(row, CORES * SLOTS) >= SLOTS).astype(jnp.int32)
    hot_core = jnp.where(where_ref[1] == 1, where_ref[0], 1 - where_ref[0])
    lent = (lax.rem(row, SLOTS) == SLOTS - 1) & (where_ref[1] != 0)
    return jnp.where(lent, hot_core, at) == core


def contract(blocks_ref, own_ref, other_ref, where_ref):
    def product(weight_ref):
        return sum(mm_t(blocks_ref[q], weight_ref[:, span]) for q, span in column_blocks(blocks_ref))

    own = product(own_ref)
    return jnp.where(rows_of_core(where_ref, own.shape, where_ref[0]), own, product(other_ref))


def expand(value, own_ref, other_ref, where_ref, out_ref):
    owned = rows_of_core(where_ref, value.shape, where_ref[0])
    mine = jnp.where(owned, value, jnp.zeros_like(value))
    theirs = jnp.where(owned, jnp.zeros_like(value), value)
    for q, span in column_blocks(out_ref):
        out_ref[q] = (mm(mine, own_ref[:, span]) + mm(theirs, other_ref[:, span])).astype(BF)


def forward_kernel(
    where_ref, rows_ref, in_ref, out_ref, other_in_ref, other_out_ref, partial_ref, proj_ref
):
    quarter = out_ref.shape[0]
    projected = contract(rows_ref, in_ref, other_in_ref, where_ref)
    proj_ref[...] = projected
    swish_value, _ = swish_parts(projected[:, :quarter])
    hidden = (swish_value * projected[:, quarter:]).astype(BF)
    expand(hidden, out_ref, other_out_ref, where_ref, partial_ref)


def backward_kernel(
    where_ref, cot_ref, proj_ref, in_ref, out_ref, other_in_ref, other_out_ref, partial_ref, pre_ref
):
    quarter = out_ref.shape[0]
    back_hidden = contract(cot_ref, out_ref, other_out_ref, where_ref)
    projected = proj_ref[...]
    swish_value, swish_slope = swish_parts(projected[:, :quarter])
    grad_pre = jnp.concatenate(
        [back_hidden * projected[:, quarter:] * swish_slope, back_hidden * swish_value], axis=1
    ).astype(BF)
    pre_ref[...] = grad_pre
    expand(grad_pre, in_ref, other_in_ref, where_ref, partial_ref)


def lent_gradient_kernel(where_ref, rows_ref, pre_ref, out_ref):
    pre = pre_ref[...]
    owned = rows_of_core(where_ref, pre.shape, where_ref[0])
    theirs = jnp.where(owned, jnp.zeros_like(pre), pre)
    for q, span in column_blocks(rows_ref):
        out_ref[:, span] = t_mm(theirs, rows_ref[q]).astype(BF)


def gradient_kernel(where_ref, rows_ref, pre_ref, lent_ref, out_ref, done_ref):
    pre = pre_ref[...]
    owned = rows_of_core(where_ref, pre.shape, where_ref[0])
    mine = jnp.where(owned, pre, jnp.zeros_like(pre))
    for q, span in column_blocks(rows_ref):
        out_ref[:, span] = (t_mm(mine, rows_ref[q]) + lent_ref[:, span].astype(F32)).astype(BF)
    done_ref[...] = jnp.zeros_like(done_ref)


def places(slot_ref, slots):
    shape = (slots, slot_ref.shape[1])
    row = lax.broadcasted_iota(jnp.int32, shape, 0)
    return [(row == slot_ref[k : k + 1, :]).astype(BF) for k in range(slot_ref.shape[0])]


def send_kernel(experts, routes_ref, tokens_ref, slot_ref, busiest_ref, out_ref):
    choices, local_tokens = routes_ref.shape
    square = (local_tokens, local_tokens)
    earlier = (
        lax.broadcasted_iota(jnp.int32, square, 0) < lax.broadcasted_iota(jnp.int32, square, 1)
    ).astype(BF)
    ids = lax.broadcasted_iota(jnp.int32, (experts, local_tokens), 0)
    counts = jnp.zeros((experts, 1), F32)
    for k in range(choices):
        expert = routes_ref[k : k + 1, :]
        member = ids == expert
        before = mm(member.astype(BF), earlier) + counts
        rank = jnp.sum(jnp.where(member, before, 0.0), axis=0, keepdims=True).astype(jnp.int32)
        counts += jnp.sum(member.astype(F32), axis=1, keepdims=True)
        slot_ref[k : k + 1, :] = jnp.where(
            rank == SLOTS, (expert ^ 1) * SLOTS + SLOTS - 1, expert * SLOTS + rank
        )
    most = jnp.max(counts, axis=0, keepdims=True)
    ids = lax.broadcasted_iota(jnp.int32, counts.shape, 0).astype(F32)
    busiest = jnp.sum(jnp.where(counts == most, ids, 0.0), axis=0, keepdims=True)
    busiest_ref[...] = busiest.astype(jnp.int32)
    both = sum(places(slot_ref, out_ref.shape[0]))
    out_ref[...] = mm(both, tokens_ref[...]).astype(BF).reshape(out_ref.shape)


def combine_kernel(slot_ref, route_weight_ref, loss_weight_ref, returned_ref, out_ref):
    place = places(slot_ref, out_ref.shape[0])
    choices = len(place)
    scales = jnp.transpose(
        jnp.concatenate(
            [route_weight_ref[...], loss_weight_ref[...], jnp.zeros((7 - choices, route_weight_ref.shape[1]), F32)], axis=0
        )
    )
    weights = [scales[:, k : k + 1] for k in range(choices)]
    returned = returned_ref[...]
    combined = sum(weights[k] * t_mm(place[k], returned) for k in range(choices))
    loss = scales[:, choices : choices + 1]
    out_ref[...] = sum(
        mm(place[k], (loss * weights[k] * combined).astype(BF)) for k in range(choices)
    ).astype(BF).reshape(out_ref.shape)


def collect_kernel(slot_ref, returned_ref, done_ref, out_ref):
    del done_ref
    both = sum(places(slot_ref, returned_ref.shape[0]))
    collected = t_mm(both, returned_ref[...]).astype(BF)
    for q in range(out_ref.shape[0]):
        out_ref[q] = collected


def join_kernel(parts_ref, out_ref):
    for q, span in column_blocks(parts_ref):
        out_ref[:, span] = parts_ref[q]


def sum_kernel(blocks_ref, out_ref):
    total = blocks_ref[0].astype(F32)
    for q in range(1, blocks_ref.shape[0]):
        total = total + blocks_ref[q].astype(F32)
    out_ref[...] = total.astype(BF).reshape(out_ref.shape)


def call(kernel, outs, args, scalars=0):
    return pl.pallas_call(
        kernel,
        out_shape=outs,
        in_specs=[SMEM] * scalars + [VMEM] * (len(args) - scalars),
        out_specs=jax.tree.map(lambda _: VMEM, outs),
        compiler_params=pltpu.CompilerParams(vmem_limit_bytes=VMEM_BYTES),
    )(*args)


def local(tokens, routes, route_weights, loss_weights, gate_up, down_weight):
    experts = lax.axis_size("expert")
    parts = lax.axis_size("dp")
    index = lax.axis_index("expert")
    local_tokens, width = tokens.shape
    cols = width // parts
    choices = routes.shape[1]
    quarter = down_weight.shape[1]
    slots = experts * SLOTS
    own_in = gate_up.reshape(2 * quarter, width)
    own_out = down_weight.reshape(quarter, width)

    def out(*shape, dtype=BF):
        return jax.ShapeDtypeStruct(shape, dtype)

    sent = out(slots, cols // LANES, LANES)
    mine = lax.dynamic_slice(
        tokens, (jnp.int32(0), lax.axis_index("dp") * cols), (local_tokens, cols)
    )
    slot, busiest, outgoing = call(
        functools.partial(send_kernel, experts),
        [out(choices, local_tokens, dtype=jnp.int32), out(1, 1, dtype=jnp.int32), sent],
        (routes.T, mine),
    )
    busiest = busiest[0, 0]
    hot = jnp.where(busiest == index, 1, jnp.where(busiest == (index ^ 1), 2, 0))
    where = jnp.stack([index & 1, hot]).astype(jnp.int32)

    other_in, other_out = swap_cores(own_in), swap_cores(own_out)
    weights = (own_in, own_out, other_in, other_out)
    rows = gather_dp(over_chips(outgoing))
    partial, projected = call(
        forward_kernel,
        [out(parts, slots, cols), out(slots, 2 * quarter, dtype=F32)],
        (where, rows, *weights),
        scalars=1,
    )
    returned = over_chips(call(sum_kernel, sent, (over_dp(partial),)))
    cot_send = call(
        combine_kernel,
        sent,
        (slot, route_weights.T, loss_weights.reshape(1, local_tokens), returned),
    )
    cot = gather_dp(over_chips(cot_send))
    input_partial, grad_pre = call(
        backward_kernel,
        [out(parts, slots, cols), out(slots, 2 * quarter)],
        (where, cot, projected, *weights),
        scalars=1,
    )
    lent = call(
        lent_gradient_kernel, out(2 * quarter, width), (where, rows, grad_pre), scalars=1
    )
    gradient, gradient_done = call(
        gradient_kernel,
        [out(2 * quarter, width), out(8, LANES, dtype=F32)],
        (where, rows, grad_pre, swap_cores(lent)),
        scalars=1,
    )
    returned_in = over_chips(call(sum_kernel, sent, (over_dp(input_partial),)))
    collected = call(
        collect_kernel, out(parts, local_tokens, cols), (slot, returned_in, gradient_done)
    )
    input_gradient = call(
        join_kernel, out(local_tokens, width), (over_dp(collected),)
    )
    return (input_gradient, gradient.reshape(1, 2, quarter, width))


def solution(mesh):
    in_specs = (
        P("expert", None),
        P("expert", None),
        P("expert", None),
        P("expert"),
        P("expert", None, "dp", None),
        P("expert", "dp", None),
    )
    out_specs = (P("expert", None), P("expert", None, "dp", None))
    return jax.shard_map(local, mesh=mesh, in_specs=in_specs, out_specs=out_specs, check_vma=False)
```

```python
import functools

import jax
import jax.numpy as jnp
from jax import lax
from jax.experimental import pallas as pl
from jax.experimental.pallas import tpu as pltpu
from jax.sharding import PartitionSpec as P

BF = jnp.bfloat16
F32 = jnp.float32
CORES = 2
SLOTS = 3
LANES = 128
VMEM_BYTES = 20 * 1024 * 1024
VMEM = pl.BlockSpec(memory_space=pltpu.VMEM)
SMEM = pl.BlockSpec(memory_space=pltpu.SMEM)


def swish_parts(preact):
    sigmoid_part = jax.nn.sigmoid(preact)
    return (preact * sigmoid_part, sigmoid_part * (1.0 + preact * (1.0 - sigmoid_part)))


def over_chips(rows):
    count = rows.shape[0]
    cols = rows.size // count
    experts = lax.axis_size("expert")
    chips = experts // CORES
    moved = lax.all_to_all(
        rows.reshape(chips, CORES * SLOTS, cols // LANES, LANES),
        "expert",
        split_axis=0,
        concat_axis=0,
        tiled=True,
        axis_index_groups=[list(range(core, experts, CORES)) for core in range(CORES)],
    )
    return moved.reshape(count, cols)


def over_dp(blocks):
    return lax.all_to_all(blocks, "dp", split_axis=0, concat_axis=0, tiled=True)


def gather_dp(block):
    return over_dp(jnp.broadcast_to(block[None], (lax.axis_size("dp"),) + block.shape))


def sum_dp(blocks):
    moved = over_dp(blocks)
    total = moved[0].astype(F32)
    for q in range(1, moved.shape[0]):
        total = total + moved[q].astype(F32)
    return total.astype(BF)


def swap_cores(value):
    experts = lax.axis_size("expert")
    return lax.ppermute(value, "expert", [(i, i ^ 1) for i in range(experts)])


def mm(a, b):
    return jnp.dot(a, b, preferred_element_type=F32)


def mm_t(a, b):
    return lax.dot_general(a, b, (((1,), (1,)), ((), ())), preferred_element_type=F32)


def t_mm(a, b):
    return lax.dot_general(a, b, (((0,), (0,)), ((), ())), preferred_element_type=F32)


def column_blocks(ref):
    parts, _, cols = ref.shape
    return [(q, slice(q * cols, (q + 1) * cols)) for q in range(parts)]


def rows_of_core(where_ref, shape, core):
    row = lax.broadcasted_iota(jnp.int32, shape, 0)
    at = (lax.rem(row, CORES * SLOTS) >= SLOTS).astype(jnp.int32)
    hot_core = jnp.where(where_ref[1] == 1, where_ref[0], 1 - where_ref[0])
    lent = (lax.rem(row, SLOTS) == SLOTS - 1) & (where_ref[1] != 0)
    return jnp.where(lent, hot_core, at) == core


def contract(blocks_ref, own_ref, other_ref, where_ref):
    def product(weight_ref):
        return sum(mm_t(blocks_ref[q], weight_ref[:, span]) for q, span in column_blocks(blocks_ref))

    own = product(own_ref)
    return jnp.where(rows_of_core(where_ref, own.shape, where_ref[0]), own, product(other_ref))


def expand(value, own_ref, other_ref, where_ref, out_ref):
    owned = rows_of_core(where_ref, value.shape, where_ref[0])
    mine = jnp.where(owned, value, jnp.zeros_like(value))
    theirs = jnp.where(owned, jnp.zeros_like(value), value)
    for q, span in column_blocks(out_ref):
        out_ref[q] = (mm(mine, own_ref[:, span]) + mm(theirs, other_ref[:, span])).astype(BF)


def forward_kernel(
    where_ref, rows_ref, in_ref, out_ref, other_in_ref, other_out_ref, partial_ref, proj_ref
):
    quarter = out_ref.shape[0]
    projected = contract(rows_ref, in_ref, other_in_ref, where_ref)
    proj_ref[...] = projected
    swish_value, _ = swish_parts(projected[:, :quarter])
    hidden = (swish_value * projected[:, quarter:]).astype(BF)
    expand(hidden, out_ref, other_out_ref, where_ref, partial_ref)


def backward_kernel(
    where_ref, cot_ref, proj_ref, in_ref, out_ref, other_in_ref, other_out_ref, partial_ref, pre_ref
):
    quarter = out_ref.shape[0]
    back_hidden = contract(cot_ref, out_ref, other_out_ref, where_ref)
    projected = proj_ref[...]
    swish_value, swish_slope = swish_parts(projected[:, :quarter])
    grad_pre = jnp.concatenate(
        [back_hidden * projected[:, quarter:] * swish_slope, back_hidden * swish_value], axis=1
    ).astype(BF)
    pre_ref[...] = grad_pre
    expand(grad_pre, in_ref, other_in_ref, where_ref, partial_ref)


def lent_gradient_kernel(where_ref, rows_ref, pre_ref, out_ref):
    pre = pre_ref[...]
    owned = rows_of_core(where_ref, pre.shape, where_ref[0])
    theirs = jnp.where(owned, jnp.zeros_like(pre), pre)
    for q, span in column_blocks(rows_ref):
        out_ref[:, span] = t_mm(theirs, rows_ref[q]).astype(BF)


def gradient_kernel(where_ref, rows_ref, pre_ref, lent_ref, out_ref, done_ref):
    pre = pre_ref[...]
    owned = rows_of_core(where_ref, pre.shape, where_ref[0])
    mine = jnp.where(owned, pre, jnp.zeros_like(pre))
    for q, span in column_blocks(rows_ref):
        out_ref[:, span] = (t_mm(mine, rows_ref[q]) + lent_ref[:, span].astype(F32)).astype(BF)
    done_ref[...] = jnp.zeros_like(done_ref)


def places(slot_ref, slots):
    shape = (slots, slot_ref.shape[1])
    row = lax.broadcasted_iota(jnp.int32, shape, 0)
    return [(row == slot_ref[k : k + 1, :]).astype(BF) for k in range(slot_ref.shape[0])]


def send_kernel(experts, routes_ref, tokens_ref, slot_ref, busiest_ref, out_ref):
    choices, local_tokens = routes_ref.shape
    square = (local_tokens, local_tokens)
    earlier = (
        lax.broadcasted_iota(jnp.int32, square, 0) < lax.broadcasted_iota(jnp.int32, square, 1)
    ).astype(BF)
    ids = lax.broadcasted_iota(jnp.int32, (experts, local_tokens), 0)
    counts = jnp.zeros((experts, 1), F32)
    for k in range(choices):
        expert = routes_ref[k : k + 1, :]
        member = ids == expert
        before = mm(member.astype(BF), earlier) + counts
        rank = jnp.sum(jnp.where(member, before, 0.0), axis=0, keepdims=True).astype(jnp.int32)
        counts += jnp.sum(member.astype(F32), axis=1, keepdims=True)
        slot_ref[k : k + 1, :] = jnp.where(
            rank == SLOTS, (expert ^ 1) * SLOTS + SLOTS - 1, expert * SLOTS + rank
        )
    most = jnp.max(counts, axis=0, keepdims=True)
    ids = lax.broadcasted_iota(jnp.int32, counts.shape, 0).astype(F32)
    busiest = jnp.sum(jnp.where(counts == most, ids, 0.0), axis=0, keepdims=True)
    busiest_ref[...] = busiest.astype(jnp.int32)
    both = sum(places(slot_ref, out_ref.shape[0]))
    out_ref[...] = mm(both, tokens_ref[...]).astype(BF).reshape(out_ref.shape)


def combine_kernel(slot_ref, route_weight_ref, loss_weight_ref, returned_ref, out_ref):
    place = places(slot_ref, out_ref.shape[0])
    choices = len(place)
    scales = jnp.transpose(
        jnp.concatenate(
            [route_weight_ref[...], loss_weight_ref[...], jnp.zeros((7 - choices, route_weight_ref.shape[1]), F32)], axis=0
        )
    )
    weights = [scales[:, k : k + 1] for k in range(choices)]
    returned = returned_ref[...]
    combined = sum(weights[k] * t_mm(place[k], returned) for k in range(choices))
    loss = scales[:, choices : choices + 1]
    out_ref[...] = sum(
        mm(place[k], (loss * weights[k] * combined).astype(BF)) for k in range(choices)
    ).astype(BF).reshape(out_ref.shape)


def collect_kernel(slot_ref, returned_ref, done_ref, out_ref):
    del done_ref
    both = sum(places(slot_ref, returned_ref.shape[0]))
    collected = t_mm(both, returned_ref[...]).astype(BF)
    for q in range(out_ref.shape[0]):
        out_ref[q] = collected


def join_kernel(parts_ref, out_ref):
    for q, span in column_blocks(parts_ref):
        out_ref[:, span] = parts_ref[q]


def sum_kernel(blocks_ref, out_ref):
    total = blocks_ref[0].astype(F32)
    for q in range(1, blocks_ref.shape[0]):
        total = total + blocks_ref[q].astype(F32)
    out_ref[...] = total.astype(BF).reshape(out_ref.shape)


def call(kernel, outs, args, scalars=0):
    return pl.pallas_call(
        kernel,
        out_shape=outs,
        in_specs=[SMEM] * scalars + [VMEM] * (len(args) - scalars),
        out_specs=jax.tree.map(lambda _: VMEM, outs),
        compiler_params=pltpu.CompilerParams(vmem_limit_bytes=VMEM_BYTES),
    )(*args)


def local(tokens, routes, route_weights, loss_weights, gate_up, down_weight):
    experts = lax.axis_size("expert")
    parts = lax.axis_size("dp")
    index = lax.axis_index("expert")
    local_tokens, width = tokens.shape
    cols = width // parts
    choices = routes.shape[1]
    quarter = down_weight.shape[1]
    slots = experts * SLOTS
    own_in = gate_up.reshape(2 * quarter, width)
    own_out = down_weight.reshape(quarter, width)

    def out(*shape, dtype=BF):
        return jax.ShapeDtypeStruct(shape, dtype)

    sent = out(slots, cols // LANES, LANES)
    mine = lax.dynamic_slice(
        tokens, (jnp.int32(0), lax.axis_index("dp") * cols), (local_tokens, cols)
    )
    slot, busiest, outgoing = call(
        functools.partial(send_kernel, experts),
        [out(choices, local_tokens, dtype=jnp.int32), out(1, 1, dtype=jnp.int32), sent],
        (routes.T, mine),
    )
    busiest = busiest[0, 0]
    hot = jnp.where(busiest == index, 1, jnp.where(busiest == (index ^ 1), 2, 0))
    where = jnp.stack([index & 1, hot]).astype(jnp.int32)

    other_in, other_out = swap_cores(own_in), swap_cores(own_out)
    weights = (own_in, own_out, other_in, other_out)
    rows = gather_dp(over_chips(outgoing))
    partial, projected = call(
        forward_kernel,
        [out(parts, slots, cols), out(slots, 2 * quarter, dtype=F32)],
        (where, rows, *weights),
        scalars=1,
    )
    returned = over_chips(call(sum_kernel, sent, (over_dp(partial),)))
    cot_send = call(
        combine_kernel,
        sent,
        (slot, route_weights.T, loss_weights.reshape(1, local_tokens), returned),
    )
    cot = gather_dp(over_chips(cot_send))
    input_partial, grad_pre = call(
        backward_kernel,
        [out(parts, slots, cols), out(slots, 2 * quarter)],
        (where, cot, projected, *weights),
        scalars=1,
    )
    lent = call(
        lent_gradient_kernel, out(2 * quarter, width), (where, rows, grad_pre), scalars=1
    )
    gradient, gradient_done = call(
        gradient_kernel,
        [out(2 * quarter, width), out(8, LANES, dtype=F32)],
        (where, rows, grad_pre, swap_cores(lent)),
        scalars=1,
    )
    returned_in = over_chips(sum_dp(input_partial))
    collected = call(
        collect_kernel, out(parts, local_tokens, cols), (slot, returned_in, gradient_done)
    )
    input_gradient = call(
        join_kernel, out(local_tokens, width), (over_dp(collected),)
    )
    return (input_gradient, gradient.reshape(1, 2, quarter, width))


def solution(mesh):
    in_specs = (
        P("expert", None),
        P("expert", None),
        P("expert", None),
        P("expert"),
        P("expert", None, "dp", None),
        P("expert", "dp", None),
    )
    out_specs = (P("expert", None), P("expert", None, "dp", None))
    return jax.shard_map(local, mesh=mesh, in_specs=in_specs, out_specs=out_specs, check_vma=False)
```

```python
import functools

import jax
import jax.numpy as jnp
from jax import lax
from jax.experimental import pallas as pl
from jax.experimental.pallas import tpu as pltpu
from jax.sharding import PartitionSpec as P

BF = jnp.bfloat16
F32 = jnp.float32
CORES = 2
SLOTS = 3
LANES = 128
VMEM_BYTES = 20 * 1024 * 1024
VMEM = pl.BlockSpec(memory_space=pltpu.VMEM)
SMEM = pl.BlockSpec(memory_space=pltpu.SMEM)
HBM = pl.BlockSpec(memory_space=pltpu.HBM)


def swish_parts(preact):
    sigmoid_part = jax.nn.sigmoid(preact)
    return (preact * sigmoid_part, sigmoid_part * (1.0 + preact * (1.0 - sigmoid_part)))


def over_chips(rows):
    count = rows.shape[0]
    cols = rows.size // count
    experts = lax.axis_size("expert")
    chips = experts // CORES
    moved = lax.all_to_all(
        rows.reshape(chips, CORES * SLOTS, cols // LANES, LANES),
        "expert",
        split_axis=0,
        concat_axis=0,
        tiled=True,
        axis_index_groups=[list(range(core, experts, CORES)) for core in range(CORES)],
    )
    return moved.reshape(count, cols)


def over_dp(blocks):
    return lax.all_to_all(blocks, "dp", split_axis=0, concat_axis=0, tiled=True)


def gather_dp(block):
    return over_dp(jnp.broadcast_to(block[None], (lax.axis_size("dp"),) + block.shape))


def sum_dp(blocks):
    moved = over_dp(blocks)
    total = moved[0].astype(F32)
    for q in range(1, moved.shape[0]):
        total = total + moved[q].astype(F32)
    return total.astype(BF)


def swap_cores(value):
    experts = lax.axis_size("expert")
    return lax.ppermute(value, "expert", [(i, i ^ 1) for i in range(experts)])


def mm(a, b):
    return jnp.dot(a, b, preferred_element_type=F32)


def mm_t(a, b):
    return lax.dot_general(a, b, (((1,), (1,)), ((), ())), preferred_element_type=F32)


def t_mm(a, b):
    return lax.dot_general(a, b, (((0,), (0,)), ((), ())), preferred_element_type=F32)


def column_blocks(ref):
    parts, _, cols = ref.shape
    return [(q, slice(q * cols, (q + 1) * cols)) for q in range(parts)]


def rows_of_core(where_ref, shape, core):
    row = lax.broadcasted_iota(jnp.int32, shape, 0)
    at = (lax.rem(row, CORES * SLOTS) >= SLOTS).astype(jnp.int32)
    hot_core = jnp.where(where_ref[1] == 1, where_ref[0], 1 - where_ref[0])
    lent = (lax.rem(row, SLOTS) == SLOTS - 1) & (where_ref[1] != 0)
    return jnp.where(lent, hot_core, at) == core


def fetch(sources, targets, sems):
    copies = [
        pltpu.make_async_copy(source, target, sems.at[i])
        for i, (source, target) in enumerate(zip(sources, targets))
    ]
    for copy in copies:
        copy.start()
    return copies


def contract(blocks_ref, own_ref, other_ref, where_ref, other_copy):
    def product(weight_ref):
        return sum(mm_t(blocks_ref[q], weight_ref[:, span]) for q, span in column_blocks(blocks_ref))

    own = product(own_ref)
    other_copy.wait()
    return jnp.where(rows_of_core(where_ref, own.shape, where_ref[0]), own, product(other_ref))


def expand(value, own_ref, other_ref, where_ref, out_ref):
    owned = rows_of_core(where_ref, value.shape, where_ref[0])
    mine = jnp.where(owned, value, jnp.zeros_like(value))
    theirs = jnp.where(owned, jnp.zeros_like(value), value)
    for q, span in column_blocks(out_ref):
        out_ref[q] = (mm(mine, own_ref[:, span]) + mm(theirs, other_ref[:, span])).astype(BF)


def forward_kernel(
    where_ref, rows_ref, in_ref, out_ref, in_far, out_far, partial_ref, proj_ref, *held
):
    other_in_ref, other_out_ref, sems = held
    in_copy, out_copy = fetch((in_far, out_far), (other_in_ref, other_out_ref), sems)
    quarter = out_ref.shape[0]
    projected = contract(rows_ref, in_ref, other_in_ref, where_ref, in_copy)
    proj_ref[...] = projected
    swish_value, _ = swish_parts(projected[:, :quarter])
    hidden = (swish_value * projected[:, quarter:]).astype(BF)
    out_copy.wait()
    expand(hidden, out_ref, other_out_ref, where_ref, partial_ref)


def backward_kernel(
    where_ref, cot_ref, proj_ref, in_ref, out_ref, in_far, out_far, partial_ref, pre_ref, *held
):
    other_in_ref, other_out_ref, sems = held
    out_copy, in_copy = fetch((out_far, in_far), (other_out_ref, other_in_ref), sems)
    quarter = out_ref.shape[0]
    back_hidden = contract(cot_ref, out_ref, other_out_ref, where_ref, out_copy)
    projected = proj_ref[...]
    swish_value, swish_slope = swish_parts(projected[:, :quarter])
    grad_pre = jnp.concatenate(
        [back_hidden * projected[:, quarter:] * swish_slope, back_hidden * swish_value], axis=1
    ).astype(BF)
    pre_ref[...] = grad_pre
    in_copy.wait()
    expand(grad_pre, in_ref, other_in_ref, where_ref, partial_ref)


def lent_gradient_kernel(where_ref, rows_ref, pre_ref, out_ref):
    pre = pre_ref[...]
    owned = rows_of_core(where_ref, pre.shape, where_ref[0])
    theirs = jnp.where(owned, jnp.zeros_like(pre), pre)
    for q, span in column_blocks(rows_ref):
        out_ref[:, span] = t_mm(theirs, rows_ref[q]).astype(BF)


def gradient_kernel(where_ref, rows_ref, pre_ref, lent_ref, out_ref, done_ref):
    pre = pre_ref[...]
    owned = rows_of_core(where_ref, pre.shape, where_ref[0])
    mine = jnp.where(owned, pre, jnp.zeros_like(pre))
    for q, span in column_blocks(rows_ref):
        out_ref[:, span] = (t_mm(mine, rows_ref[q]) + lent_ref[:, span].astype(F32)).astype(BF)
    done_ref[...] = jnp.zeros_like(done_ref)


def places(slot_ref, slots):
    shape = (slots, slot_ref.shape[1])
    row = lax.broadcasted_iota(jnp.int32, shape, 0)
    return [(row == slot_ref[k : k + 1, :]).astype(BF) for k in range(slot_ref.shape[0])]


def send_kernel(experts, routes_ref, tokens_ref, slot_ref, busiest_ref, out_ref):
    choices, local_tokens = routes_ref.shape
    square = (local_tokens, local_tokens)
    earlier = (
        lax.broadcasted_iota(jnp.int32, square, 0) < lax.broadcasted_iota(jnp.int32, square, 1)
    ).astype(BF)
    ids = lax.broadcasted_iota(jnp.int32, (experts, local_tokens), 0)
    counts = jnp.zeros((experts, 1), F32)
    for k in range(choices):
        expert = routes_ref[k : k + 1, :]
        member = ids == expert
        before = mm(member.astype(BF), earlier) + counts
        rank = jnp.sum(jnp.where(member, before, 0.0), axis=0, keepdims=True).astype(jnp.int32)
        counts += jnp.sum(member.astype(F32), axis=1, keepdims=True)
        slot_ref[k : k + 1, :] = jnp.where(
            rank == SLOTS, (expert ^ 1) * SLOTS + SLOTS - 1, expert * SLOTS + rank
        )
    most = jnp.max(counts, axis=0, keepdims=True)
    ids = lax.broadcasted_iota(jnp.int32, counts.shape, 0).astype(F32)
    busiest = jnp.sum(jnp.where(counts == most, ids, 0.0), axis=0, keepdims=True)
    busiest_ref[...] = busiest.astype(jnp.int32)
    both = sum(places(slot_ref, out_ref.shape[0]))
    out_ref[...] = mm(both, tokens_ref[...]).astype(BF).reshape(out_ref.shape)


def combine_kernel(slot_ref, route_weight_ref, loss_weight_ref, returned_ref, out_ref):
    place = places(slot_ref, out_ref.shape[0])
    choices = len(place)
    scales = jnp.transpose(
        jnp.concatenate(
            [route_weight_ref[...], loss_weight_ref[...], jnp.zeros((7 - choices, route_weight_ref.shape[1]), F32)], axis=0
        )
    )
    weights = [scales[:, k : k + 1] for k in range(choices)]
    returned = returned_ref[...]
    combined = sum(weights[k] * t_mm(place[k], returned) for k in range(choices))
    loss = scales[:, choices : choices + 1]
    out_ref[...] = sum(
        mm(place[k], (loss * weights[k] * combined).astype(BF)) for k in range(choices)
    ).astype(BF).reshape(out_ref.shape)


def collect_kernel(slot_ref, returned_ref, done_ref, out_ref):
    del done_ref
    both = sum(places(slot_ref, returned_ref.shape[0]))
    collected = t_mm(both, returned_ref[...]).astype(BF)
    for q in range(out_ref.shape[0]):
        out_ref[q] = collected


def join_kernel(parts_ref, out_ref):
    for q, span in column_blocks(parts_ref):
        out_ref[:, span] = parts_ref[q]


def sum_kernel(blocks_ref, out_ref):
    total = blocks_ref[0].astype(F32)
    for q in range(1, blocks_ref.shape[0]):
        total = total + blocks_ref[q].astype(F32)
    out_ref[...] = total.astype(BF).reshape(out_ref.shape)


def call(kernel, outs, args, scalars=0, far=0, scratch=()):
    near = len(args) - scalars - far
    return pl.pallas_call(
        kernel,
        out_shape=outs,
        in_specs=[SMEM] * scalars + [VMEM] * near + [HBM] * far,
        out_specs=jax.tree.map(lambda _: VMEM, outs),
        scratch_shapes=list(scratch),
        compiler_params=pltpu.CompilerParams(vmem_limit_bytes=VMEM_BYTES),
    )(*args)


def local(tokens, routes, route_weights, loss_weights, gate_up, down_weight):
    experts = lax.axis_size("expert")
    parts = lax.axis_size("dp")
    index = lax.axis_index("expert")
    local_tokens, width = tokens.shape
    cols = width // parts
    choices = routes.shape[1]
    quarter = down_weight.shape[1]
    slots = experts * SLOTS
    own_in = gate_up.reshape(2 * quarter, width)
    own_out = down_weight.reshape(quarter, width)

    def out(*shape, dtype=BF):
        return jax.ShapeDtypeStruct(shape, dtype)

    sent = out(slots, cols // LANES, LANES)
    mine = lax.dynamic_slice(
        tokens, (jnp.int32(0), lax.axis_index("dp") * cols), (local_tokens, cols)
    )
    slot, busiest, outgoing = call(
        functools.partial(send_kernel, experts),
        [out(choices, local_tokens, dtype=jnp.int32), out(1, 1, dtype=jnp.int32), sent],
        (routes.T, mine),
    )
    busiest = busiest[0, 0]
    hot = jnp.where(busiest == index, 1, jnp.where(busiest == (index ^ 1), 2, 0))
    where = jnp.stack([index & 1, hot]).astype(jnp.int32)

    other_in, other_out = swap_cores(own_in), swap_cores(own_out)
    weights = (own_in, own_out, other_in, other_out)
    held = [
        pltpu.VMEM(own_in.shape, BF),
        pltpu.VMEM(own_out.shape, BF),
        pltpu.SemaphoreType.DMA((2,)),
    ]
    rows = gather_dp(over_chips(outgoing))
    partial, projected = call(
        forward_kernel,
        [out(parts, slots, cols), out(slots, 2 * quarter, dtype=F32)],
        (where, rows, *weights),
        scalars=1,
        far=2,
        scratch=held,
    )
    returned = over_chips(call(sum_kernel, sent, (over_dp(partial),)))
    cot_send = call(
        combine_kernel,
        sent,
        (slot, route_weights.T, loss_weights.reshape(1, local_tokens), returned),
    )
    cot = gather_dp(over_chips(cot_send))
    input_partial, grad_pre = call(
        backward_kernel,
        [out(parts, slots, cols), out(slots, 2 * quarter)],
        (where, cot, projected, *weights),
        scalars=1,
        far=2,
        scratch=held,
    )
    lent = call(
        lent_gradient_kernel, out(2 * quarter, width), (where, rows, grad_pre), scalars=1
    )
    gradient, gradient_done = call(
        gradient_kernel,
        [out(2 * quarter, width), out(8, LANES, dtype=F32)],
        (where, rows, grad_pre, swap_cores(lent)),
        scalars=1,
    )
    returned_in = over_chips(sum_dp(input_partial))
    collected = call(
        collect_kernel, out(parts, local_tokens, cols), (slot, returned_in, gradient_done)
    )
    input_gradient = call(
        join_kernel, out(local_tokens, width), (over_dp(collected),)
    )
    return (input_gradient, gradient.reshape(1, 2, quarter, width))


def solution(mesh):
    in_specs = (
        P("expert", None),
        P("expert", None),
        P("expert", None),
        P("expert"),
        P("expert", None, "dp", None),
        P("expert", "dp", None),
    )
    out_specs = (P("expert", None), P("expert", None, "dp", None))
    return jax.shard_map(local, mesh=mesh, in_specs=in_specs, out_specs=out_specs, check_vma=False)
```

```python
import functools

import jax
import jax.numpy as jnp
from jax import lax
from jax.experimental import pallas as pl
from jax.experimental.pallas import tpu as pltpu
from jax.sharding import PartitionSpec as P

BF = jnp.bfloat16
F32 = jnp.float32
CORES = 2
SLOTS = 3
LANES = 128
VMEM_BYTES = 20 * 1024 * 1024
VMEM = pl.BlockSpec(memory_space=pltpu.VMEM)
SMEM = pl.BlockSpec(memory_space=pltpu.SMEM)
HBM = pl.BlockSpec(memory_space=pltpu.HBM)


def swish_parts(preact):
    sigmoid_part = jax.nn.sigmoid(preact)
    return (preact * sigmoid_part, sigmoid_part * (1.0 + preact * (1.0 - sigmoid_part)))


def over_chips(rows):
    count = rows.shape[0]
    cols = rows.size // count
    experts = lax.axis_size("expert")
    chips = experts // CORES
    moved = lax.all_to_all(
        rows.reshape(chips, CORES * SLOTS, cols // LANES, LANES),
        "expert",
        split_axis=0,
        concat_axis=0,
        tiled=True,
        axis_index_groups=[list(range(core, experts, CORES)) for core in range(CORES)],
    )
    return moved.reshape(count, cols)


def over_dp(blocks):
    return lax.all_to_all(blocks, "dp", split_axis=0, concat_axis=0, tiled=True)


def gather_dp(block):
    return over_dp(jnp.broadcast_to(block[None], (lax.axis_size("dp"),) + block.shape))


def sum_dp(blocks):
    moved = over_dp(blocks)
    total = moved[0].astype(F32)
    for q in range(1, moved.shape[0]):
        total = total + moved[q].astype(F32)
    return total.astype(BF)


def swap_cores(value):
    experts = lax.axis_size("expert")
    return lax.ppermute(value, "expert", [(i, i ^ 1) for i in range(experts)])


def mm(a, b):
    return jnp.dot(a, b, preferred_element_type=F32)


def mm_t(a, b):
    return lax.dot_general(a, b, (((1,), (1,)), ((), ())), preferred_element_type=F32)


def t_mm(a, b):
    return lax.dot_general(a, b, (((0,), (0,)), ((), ())), preferred_element_type=F32)


def column_blocks(ref):
    parts, _, cols = ref.shape
    return [(q, slice(q * cols, (q + 1) * cols)) for q in range(parts)]


def rows_of_core(where_ref, shape, core):
    row = lax.broadcasted_iota(jnp.int32, shape, 0)
    at = (lax.rem(row, CORES * SLOTS) >= SLOTS).astype(jnp.int32)
    hot_core = jnp.where(where_ref[1] == 1, where_ref[0], 1 - where_ref[0])
    lent = (lax.rem(row, SLOTS) == SLOTS - 1) & (where_ref[1] != 0)
    return jnp.where(lent, hot_core, at) == core


def fetch(sources, targets, sems):
    copies = [
        pltpu.make_async_copy(source, target, sems.at[i])
        for i, (source, target) in enumerate(zip(sources, targets))
    ]
    for copy in copies:
        copy.start()
    return copies


def contract(blocks_ref, own_ref, other_ref, where_ref, other_copy=None):
    def product(weight_ref):
        return sum(mm_t(blocks_ref[q], weight_ref[:, span]) for q, span in column_blocks(blocks_ref))

    own = product(own_ref)
    if other_copy is not None:
        other_copy.wait()
    return jnp.where(rows_of_core(where_ref, own.shape, where_ref[0]), own, product(other_ref))


def expand(value, own_ref, other_ref, where_ref, out_ref):
    owned = rows_of_core(where_ref, value.shape, where_ref[0])
    mine = jnp.where(owned, value, jnp.zeros_like(value))
    theirs = jnp.where(owned, jnp.zeros_like(value), value)
    for q, span in column_blocks(out_ref):
        out_ref[q] = (mm(mine, own_ref[:, span]) + mm(theirs, other_ref[:, span])).astype(BF)


def forward_kernel(
    where_ref, rows_ref, in_ref, out_ref, in_far, out_far, partial_ref, proj_ref, *held
):
    other_in_ref, other_out_ref, sems = held
    in_copy, out_copy = fetch((in_far, out_far), (other_in_ref, other_out_ref), sems)
    quarter = out_ref.shape[0]
    projected = contract(rows_ref, in_ref, other_in_ref, where_ref, in_copy)
    proj_ref[...] = projected
    swish_value, _ = swish_parts(projected[:, :quarter])
    hidden = (swish_value * projected[:, quarter:]).astype(BF)
    out_copy.wait()
    expand(hidden, out_ref, other_out_ref, where_ref, partial_ref)


def backward_kernel(
    where_ref, cot_ref, proj_ref, in_ref, out_ref, other_in_ref, other_out_ref, partial_ref, pre_ref
):
    quarter = out_ref.shape[0]
    back_hidden = contract(cot_ref, out_ref, other_out_ref, where_ref)
    projected = proj_ref[...]
    swish_value, swish_slope = swish_parts(projected[:, :quarter])
    grad_pre = jnp.concatenate(
        [back_hidden * projected[:, quarter:] * swish_slope, back_hidden * swish_value], axis=1
    ).astype(BF)
    pre_ref[...] = grad_pre
    expand(grad_pre, in_ref, other_in_ref, where_ref, partial_ref)


def lent_gradient_kernel(where_ref, rows_ref, pre_ref, out_ref):
    pre = pre_ref[...]
    owned = rows_of_core(where_ref, pre.shape, where_ref[0])
    theirs = jnp.where(owned, jnp.zeros_like(pre), pre)
    for q, span in column_blocks(rows_ref):
        out_ref[:, span] = t_mm(theirs, rows_ref[q]).astype(BF)


def gradient_kernel(where_ref, rows_ref, pre_ref, lent_ref, out_ref, done_ref):
    pre = pre_ref[...]
    owned = rows_of_core(where_ref, pre.shape, where_ref[0])
    mine = jnp.where(owned, pre, jnp.zeros_like(pre))
    for q, span in column_blocks(rows_ref):
        out_ref[:, span] = (t_mm(mine, rows_ref[q]) + lent_ref[:, span].astype(F32)).astype(BF)
    done_ref[...] = jnp.zeros_like(done_ref)


def places(slot_ref, slots):
    shape = (slots, slot_ref.shape[1])
    row = lax.broadcasted_iota(jnp.int32, shape, 0)
    return [(row == slot_ref[k : k + 1, :]).astype(BF) for k in range(slot_ref.shape[0])]


def send_kernel(experts, routes_ref, tokens_ref, slot_ref, busiest_ref, out_ref):
    choices, local_tokens = routes_ref.shape
    square = (local_tokens, local_tokens)
    earlier = (
        lax.broadcasted_iota(jnp.int32, square, 0) < lax.broadcasted_iota(jnp.int32, square, 1)
    ).astype(BF)
    ids = lax.broadcasted_iota(jnp.int32, (experts, local_tokens), 0)
    counts = jnp.zeros((experts, 1), F32)
    for k in range(choices):
        expert = routes_ref[k : k + 1, :]
        member = ids == expert
        before = mm(member.astype(BF), earlier) + counts
        rank = jnp.sum(jnp.where(member, before, 0.0), axis=0, keepdims=True).astype(jnp.int32)
        counts += jnp.sum(member.astype(F32), axis=1, keepdims=True)
        slot_ref[k : k + 1, :] = jnp.where(
            rank == SLOTS, (expert ^ 1) * SLOTS + SLOTS - 1, expert * SLOTS + rank
        )
    most = jnp.max(counts, axis=0, keepdims=True)
    ids = lax.broadcasted_iota(jnp.int32, counts.shape, 0).astype(F32)
    busiest = jnp.sum(jnp.where(counts == most, ids, 0.0), axis=0, keepdims=True)
    busiest_ref[...] = busiest.astype(jnp.int32)
    both = sum(places(slot_ref, out_ref.shape[0]))
    out_ref[...] = mm(both, tokens_ref[...]).astype(BF).reshape(out_ref.shape)


def combine_kernel(slot_ref, route_weight_ref, loss_weight_ref, returned_ref, out_ref):
    place = places(slot_ref, out_ref.shape[0])
    choices = len(place)
    scales = jnp.transpose(
        jnp.concatenate(
            [route_weight_ref[...], loss_weight_ref[...], jnp.zeros((7 - choices, route_weight_ref.shape[1]), F32)], axis=0
        )
    )
    weights = [scales[:, k : k + 1] for k in range(choices)]
    returned = returned_ref[...]
    combined = sum(weights[k] * t_mm(place[k], returned) for k in range(choices))
    loss = scales[:, choices : choices + 1]
    out_ref[...] = sum(
        mm(place[k], (loss * weights[k] * combined).astype(BF)) for k in range(choices)
    ).astype(BF).reshape(out_ref.shape)


def collect_kernel(slot_ref, returned_ref, done_ref, out_ref):
    del done_ref
    both = sum(places(slot_ref, returned_ref.shape[0]))
    collected = t_mm(both, returned_ref[...]).astype(BF)
    for q in range(out_ref.shape[0]):
        out_ref[q] = collected


def join_kernel(parts_ref, out_ref):
    for q, span in column_blocks(parts_ref):
        out_ref[:, span] = parts_ref[q]


def sum_kernel(blocks_ref, out_ref):
    total = blocks_ref[0].astype(F32)
    for q in range(1, blocks_ref.shape[0]):
        total = total + blocks_ref[q].astype(F32)
    out_ref[...] = total.astype(BF).reshape(out_ref.shape)


def call(kernel, outs, args, scalars=0, far=0, scratch=()):
    near = len(args) - scalars - far
    return pl.pallas_call(
        kernel,
        out_shape=outs,
        in_specs=[SMEM] * scalars + [VMEM] * near + [HBM] * far,
        out_specs=jax.tree.map(lambda _: VMEM, outs),
        scratch_shapes=list(scratch),
        compiler_params=pltpu.CompilerParams(vmem_limit_bytes=VMEM_BYTES),
    )(*args)


def local(tokens, routes, route_weights, loss_weights, gate_up, down_weight):
    experts = lax.axis_size("expert")
    parts = lax.axis_size("dp")
    index = lax.axis_index("expert")
    local_tokens, width = tokens.shape
    cols = width // parts
    choices = routes.shape[1]
    quarter = down_weight.shape[1]
    slots = experts * SLOTS
    own_in = gate_up.reshape(2 * quarter, width)
    own_out = down_weight.reshape(quarter, width)

    def out(*shape, dtype=BF):
        return jax.ShapeDtypeStruct(shape, dtype)

    sent = out(slots, cols // LANES, LANES)
    mine = lax.dynamic_slice(
        tokens, (jnp.int32(0), lax.axis_index("dp") * cols), (local_tokens, cols)
    )
    slot, busiest, outgoing = call(
        functools.partial(send_kernel, experts),
        [out(choices, local_tokens, dtype=jnp.int32), out(1, 1, dtype=jnp.int32), sent],
        (routes.T, mine),
    )
    busiest = busiest[0, 0]
    hot = jnp.where(busiest == index, 1, jnp.where(busiest == (index ^ 1), 2, 0))
    where = jnp.stack([index & 1, hot]).astype(jnp.int32)

    other_in, other_out = swap_cores(own_in), swap_cores(own_out)
    weights = (own_in, own_out, other_in, other_out)
    held = [
        pltpu.VMEM(own_in.shape, BF),
        pltpu.VMEM(own_out.shape, BF),
        pltpu.SemaphoreType.DMA((2,)),
    ]
    rows = gather_dp(over_chips(outgoing))
    partial, projected = call(
        forward_kernel,
        [out(parts, slots, cols), out(slots, 2 * quarter, dtype=F32)],
        (where, rows, *weights),
        scalars=1,
        far=2,
        scratch=held,
    )
    returned = over_chips(call(sum_kernel, sent, (over_dp(partial),)))
    cot_send = call(
        combine_kernel,
        sent,
        (slot, route_weights.T, loss_weights.reshape(1, local_tokens), returned),
    )
    cot = gather_dp(over_chips(cot_send))
    input_partial, grad_pre = call(
        backward_kernel,
        [out(parts, slots, cols), out(slots, 2 * quarter)],
        (where, cot, projected, *weights),
        scalars=1,
    )
    lent = call(
        lent_gradient_kernel, out(2 * quarter, width), (where, rows, grad_pre), scalars=1
    )
    gradient, gradient_done = call(
        gradient_kernel,
        [out(2 * quarter, width), out(8, LANES, dtype=F32)],
        (where, rows, grad_pre, swap_cores(lent)),
        scalars=1,
    )
    returned_in = over_chips(sum_dp(input_partial))
    collected = call(
        collect_kernel, out(parts, local_tokens, cols), (slot, returned_in, gradient_done)
    )
    input_gradient = call(
        join_kernel, out(local_tokens, width), (over_dp(collected),)
    )
    return (input_gradient, gradient.reshape(1, 2, quarter, width))


def solution(mesh):
    in_specs = (
        P("expert", None),
        P("expert", None),
        P("expert", None),
        P("expert"),
        P("expert", None, "dp", None),
        P("expert", "dp", None),
    )
    out_specs = (P("expert", None), P("expert", None, "dp", None))
    return jax.shard_map(local, mesh=mesh, in_specs=in_specs, out_specs=out_specs, check_vma=False)
```

```python
import functools

import jax
import jax.numpy as jnp
from jax import lax
from jax.experimental import pallas as pl
from jax.experimental.pallas import tpu as pltpu
from jax.sharding import PartitionSpec as P

BF = jnp.bfloat16
F32 = jnp.float32
CORES = 2
SLOTS = 3
LANES = 128
VMEM_BYTES = 20 * 1024 * 1024
VMEM = pl.BlockSpec(memory_space=pltpu.VMEM)
SMEM = pl.BlockSpec(memory_space=pltpu.SMEM)
HBM = pl.BlockSpec(memory_space=pltpu.HBM)


def swish_parts(preact):
    sigmoid_part = jax.nn.sigmoid(preact)
    return (preact * sigmoid_part, sigmoid_part * (1.0 + preact * (1.0 - sigmoid_part)))


def over_chips(rows):
    count = rows.shape[0]
    cols = rows.size // count
    experts = lax.axis_size("expert")
    chips = experts // CORES
    moved = lax.all_to_all(
        rows.reshape(chips, CORES * SLOTS, cols // LANES, LANES),
        "expert",
        split_axis=0,
        concat_axis=0,
        tiled=True,
        axis_index_groups=[list(range(core, experts, CORES)) for core in range(CORES)],
    )
    return moved.reshape(count, cols)


def over_dp(blocks):
    return lax.all_to_all(blocks, "dp", split_axis=0, concat_axis=0, tiled=True)


def gather_dp(block):
    return over_dp(jnp.broadcast_to(block[None], (lax.axis_size("dp"),) + block.shape))


def sum_dp(blocks):
    moved = over_dp(blocks)
    total = moved[0].astype(F32)
    for q in range(1, moved.shape[0]):
        total = total + moved[q].astype(F32)
    return total.astype(BF)


def swap_cores(value):
    experts = lax.axis_size("expert")
    return lax.ppermute(value, "expert", [(i, i ^ 1) for i in range(experts)])


def mm(a, b):
    return jnp.dot(a, b, preferred_element_type=F32)


def mm_t(a, b):
    return lax.dot_general(a, b, (((1,), (1,)), ((), ())), preferred_element_type=F32)


def t_mm(a, b):
    return lax.dot_general(a, b, (((0,), (0,)), ((), ())), preferred_element_type=F32)


def column_blocks(ref):
    parts, _, cols = ref.shape
    return [(q, slice(q * cols, (q + 1) * cols)) for q in range(parts)]


def rows_of_core(where_ref, shape, core):
    row = lax.broadcasted_iota(jnp.int32, shape, 0)
    at = (lax.rem(row, CORES * SLOTS) >= SLOTS).astype(jnp.int32)
    hot_core = jnp.where(where_ref[1] == 1, where_ref[0], 1 - where_ref[0])
    lent = (lax.rem(row, SLOTS) == SLOTS - 1) & (where_ref[1] != 0)
    return jnp.where(lent, hot_core, at) == core


def fetch(sources, targets, sems):
    copies = [
        pltpu.make_async_copy(source, target, sems.at[i])
        for i, (source, target) in enumerate(zip(sources, targets))
    ]
    for copy in copies:
        copy.start()
    return copies


def contract(blocks_ref, own_ref, other_ref, where_ref, other_copy=None):
    def product(weight_ref):
        return sum(mm_t(blocks_ref[q], weight_ref[:, span]) for q, span in column_blocks(blocks_ref))

    own = product(own_ref)
    if other_copy is not None:
        other_copy.wait()
    return jnp.where(rows_of_core(where_ref, own.shape, where_ref[0]), own, product(other_ref))


def expand(value, own_ref, other_ref, where_ref, out_ref):
    owned = rows_of_core(where_ref, value.shape, where_ref[0])
    mine = jnp.where(owned, value, jnp.zeros_like(value))
    theirs = jnp.where(owned, jnp.zeros_like(value), value)
    for q, span in column_blocks(out_ref):
        out_ref[q] = (mm(mine, own_ref[:, span]) + mm(theirs, other_ref[:, span])).astype(BF)


def forward_kernel(
    where_ref, rows_ref, in_ref, out_ref, in_far, out_far, partial_ref, proj_ref, *held
):
    other_in_ref, other_out_ref, sems = held
    in_copy, out_copy = fetch((in_far, out_far), (other_in_ref, other_out_ref), sems)
    quarter = out_ref.shape[0]
    projected = contract(rows_ref, in_ref, other_in_ref, where_ref, in_copy)
    proj_ref[...] = projected
    swish_value, _ = swish_parts(projected[:, :quarter])
    hidden = (swish_value * projected[:, quarter:]).astype(BF)
    out_copy.wait()
    expand(hidden, out_ref, other_out_ref, where_ref, partial_ref)


def backward_kernel(
    where_ref, cot_ref, proj_ref, in_ref, out_ref, other_out_ref, in_far, partial_ref, pre_ref, *held
):
    other_in_ref, sems = held
    (in_copy,) = fetch((in_far,), (other_in_ref,), sems)
    quarter = out_ref.shape[0]
    back_hidden = contract(cot_ref, out_ref, other_out_ref, where_ref)
    projected = proj_ref[...]
    swish_value, swish_slope = swish_parts(projected[:, :quarter])
    grad_pre = jnp.concatenate(
        [back_hidden * projected[:, quarter:] * swish_slope, back_hidden * swish_value], axis=1
    ).astype(BF)
    pre_ref[...] = grad_pre
    in_copy.wait()
    expand(grad_pre, in_ref, other_in_ref, where_ref, partial_ref)


def lent_gradient_kernel(where_ref, rows_ref, pre_ref, out_ref):
    pre = pre_ref[...]
    owned = rows_of_core(where_ref, pre.shape, where_ref[0])
    theirs = jnp.where(owned, jnp.zeros_like(pre), pre)
    for q, span in column_blocks(rows_ref):
        out_ref[:, span] = t_mm(theirs, rows_ref[q]).astype(BF)


def gradient_kernel(where_ref, rows_ref, pre_ref, lent_ref, out_ref, done_ref):
    pre = pre_ref[...]
    owned = rows_of_core(where_ref, pre.shape, where_ref[0])
    mine = jnp.where(owned, pre, jnp.zeros_like(pre))
    for q, span in column_blocks(rows_ref):
        out_ref[:, span] = (t_mm(mine, rows_ref[q]) + lent_ref[:, span].astype(F32)).astype(BF)
    done_ref[...] = jnp.zeros_like(done_ref)


def places(slot_ref, slots):
    shape = (slots, slot_ref.shape[1])
    row = lax.broadcasted_iota(jnp.int32, shape, 0)
    return [(row == slot_ref[k : k + 1, :]).astype(BF) for k in range(slot_ref.shape[0])]


def send_kernel(experts, routes_ref, tokens_ref, slot_ref, busiest_ref, out_ref):
    choices, local_tokens = routes_ref.shape
    square = (local_tokens, local_tokens)
    earlier = (
        lax.broadcasted_iota(jnp.int32, square, 0) < lax.broadcasted_iota(jnp.int32, square, 1)
    ).astype(BF)
    ids = lax.broadcasted_iota(jnp.int32, (experts, local_tokens), 0)
    counts = jnp.zeros((experts, 1), F32)
    for k in range(choices):
        expert = routes_ref[k : k + 1, :]
        member = ids == expert
        before = mm(member.astype(BF), earlier) + counts
        rank = jnp.sum(jnp.where(member, before, 0.0), axis=0, keepdims=True).astype(jnp.int32)
        counts += jnp.sum(member.astype(F32), axis=1, keepdims=True)
        slot_ref[k : k + 1, :] = jnp.where(
            rank == SLOTS, (expert ^ 1) * SLOTS + SLOTS - 1, expert * SLOTS + rank
        )
    most = jnp.max(counts, axis=0, keepdims=True)
    ids = lax.broadcasted_iota(jnp.int32, counts.shape, 0).astype(F32)
    busiest = jnp.sum(jnp.where(counts == most, ids, 0.0), axis=0, keepdims=True)
    busiest_ref[...] = busiest.astype(jnp.int32)
    both = sum(places(slot_ref, out_ref.shape[0]))
    out_ref[...] = mm(both, tokens_ref[...]).astype(BF).reshape(out_ref.shape)


def combine_kernel(slot_ref, route_weight_ref, loss_weight_ref, returned_ref, out_ref):
    place = places(slot_ref, out_ref.shape[0])
    choices = len(place)
    scales = jnp.transpose(
        jnp.concatenate(
            [route_weight_ref[...], loss_weight_ref[...], jnp.zeros((7 - choices, route_weight_ref.shape[1]), F32)], axis=0
        )
    )
    weights = [scales[:, k : k + 1] for k in range(choices)]
    returned = returned_ref[...]
    combined = sum(weights[k] * t_mm(place[k], returned) for k in range(choices))
    loss = scales[:, choices : choices + 1]
    out_ref[...] = sum(
        mm(place[k], (loss * weights[k] * combined).astype(BF)) for k in range(choices)
    ).astype(BF).reshape(out_ref.shape)


def collect_kernel(slot_ref, returned_ref, done_ref, out_ref):
    del done_ref
    both = sum(places(slot_ref, returned_ref.shape[0]))
    collected = t_mm(both, returned_ref[...]).astype(BF)
    for q in range(out_ref.shape[0]):
        out_ref[q] = collected


def join_kernel(parts_ref, out_ref):
    for q, span in column_blocks(parts_ref):
        out_ref[:, span] = parts_ref[q]


def sum_kernel(blocks_ref, out_ref):
    total = blocks_ref[0].astype(F32)
    for q in range(1, blocks_ref.shape[0]):
        total = total + blocks_ref[q].astype(F32)
    out_ref[...] = total.astype(BF).reshape(out_ref.shape)


def call(kernel, outs, args, scalars=0, far=0, scratch=()):
    near = len(args) - scalars - far
    return pl.pallas_call(
        kernel,
        out_shape=outs,
        in_specs=[SMEM] * scalars + [VMEM] * near + [HBM] * far,
        out_specs=jax.tree.map(lambda _: VMEM, outs),
        scratch_shapes=list(scratch),
        compiler_params=pltpu.CompilerParams(vmem_limit_bytes=VMEM_BYTES),
    )(*args)


def local(tokens, routes, route_weights, loss_weights, gate_up, down_weight):
    experts = lax.axis_size("expert")
    parts = lax.axis_size("dp")
    index = lax.axis_index("expert")
    local_tokens, width = tokens.shape
    cols = width // parts
    choices = routes.shape[1]
    quarter = down_weight.shape[1]
    slots = experts * SLOTS
    own_in = gate_up.reshape(2 * quarter, width)
    own_out = down_weight.reshape(quarter, width)

    def out(*shape, dtype=BF):
        return jax.ShapeDtypeStruct(shape, dtype)

    sent = out(slots, cols // LANES, LANES)
    mine = lax.dynamic_slice(
        tokens, (jnp.int32(0), lax.axis_index("dp") * cols), (local_tokens, cols)
    )
    slot, busiest, outgoing = call(
        functools.partial(send_kernel, experts),
        [out(choices, local_tokens, dtype=jnp.int32), out(1, 1, dtype=jnp.int32), sent],
        (routes.T, mine),
    )
    busiest = busiest[0, 0]
    hot = jnp.where(busiest == index, 1, jnp.where(busiest == (index ^ 1), 2, 0))
    where = jnp.stack([index & 1, hot]).astype(jnp.int32)

    other_in, other_out = swap_cores(own_in), swap_cores(own_out)
    weights = (own_in, own_out, other_in, other_out)
    held = [
        pltpu.VMEM(own_in.shape, BF),
        pltpu.VMEM(own_out.shape, BF),
        pltpu.SemaphoreType.DMA((2,)),
    ]
    rows = gather_dp(over_chips(outgoing))
    partial, projected = call(
        forward_kernel,
        [out(parts, slots, cols), out(slots, 2 * quarter, dtype=F32)],
        (where, rows, *weights),
        scalars=1,
        far=2,
        scratch=held,
    )
    returned = over_chips(call(sum_kernel, sent, (over_dp(partial),)))
    cot_send = call(
        combine_kernel,
        sent,
        (slot, route_weights.T, loss_weights.reshape(1, local_tokens), returned),
    )
    cot = gather_dp(over_chips(cot_send))
    input_partial, grad_pre = call(
        backward_kernel,
        [out(parts, slots, cols), out(slots, 2 * quarter)],
        (where, cot, projected, own_in, own_out, other_out, other_in),
        scalars=1,
        far=1,
        scratch=[held[0], pltpu.SemaphoreType.DMA((1,))],
    )
    lent = call(
        lent_gradient_kernel, out(2 * quarter, width), (where, rows, grad_pre), scalars=1
    )
    gradient, gradient_done = call(
        gradient_kernel,
        [out(2 * quarter, width), out(8, LANES, dtype=F32)],
        (where, rows, grad_pre, swap_cores(lent)),
        scalars=1,
    )
    returned_in = over_chips(sum_dp(input_partial))
    collected = call(
        collect_kernel, out(parts, local_tokens, cols), (slot, returned_in, gradient_done)
    )
    input_gradient = call(
        join_kernel, out(local_tokens, width), (over_dp(collected),)
    )
    return (input_gradient, gradient.reshape(1, 2, quarter, width))


def solution(mesh):
    in_specs = (
        P("expert", None),
        P("expert", None),
        P("expert", None),
        P("expert"),
        P("expert", None, "dp", None),
        P("expert", "dp", None),
    )
    out_specs = (P("expert", None), P("expert", None, "dp", None))
    return jax.shard_map(local, mesh=mesh, in_specs=in_specs, out_specs=out_specs, check_vma=False)
```
